512 devices in a mesh: rep: 8 (over x, core), tp: 32 (over z_hi, y), fsdp: 2 (over z_lo).
Axes of the slice: x: 4, y: 8, z: 8 (z_hi: 4, z_lo: 2; z = z_hi * 2 + z_lo), core: 2. Of those that a mesh axis runs over, the one named last changes fastest.
Arguments:
- tokens: bfloat16 [4, 1024, 2048], P(None, ('rep', 'fsdp'), 'tp'), may hold values from -6 to 6
- norm_gain: bfloat16 [2048], replicated, may hold values from 0.5 to 2
- router: bfloat16 [2048, 8], replicated, may hold values from -0.125 to 0.125
- routes: int32 [4, 1024, 2], P(None, ('rep', 'fsdp')), may hold values from 0 to 7, all different within a row; in each aligned block of 64 rows (0 to 63, 64 to 127, ..., all dimensions but the last counted through in order) at most 32 rows name the same one
- expert_weights: bfloat16 [32, 2048, 768], P('tp'), may hold values from -0.125 to 0.125
- codes: bfloat16 [32, 2048, 768], P('tp', ('rep', 'fsdp')), may hold values from -6 to 6
- scales: bfloat16 [32, 2048, 48], P('tp', ('rep', 'fsdp')), may hold values from 0.0019989014 to 0.019897461
- owner_map: int32 [2048], replicated, may hold values from 0 to 2047, each once
Outputs:
- mixed: bfloat16 [4, 1024, 2048], P(None, ('rep', 'fsdp'), 'tp')
The draws below stay inside these ranges and needn't reach their ends.
Inputs may be any that keep to these rules, and one draw needn't show every extreme that they name: `owner_map`: each number appears once. `routes`: a row names 2 different experts; within one step's 64 rows of one rollout group (aligned blocks of 64 rows), no expert is named by more than 32 rows, a bound that some block reaches.
All inputs are finite; a program needn't handle non-finite values.
Results may differ from the reference program's by a relative error of at most 0.02.
Values may be sent and summed in bfloat16 or wider, within the bound.
A program may use at most 64 MiB of HBM per device.

```python
import math
import jax
import jax.numpy as jnp
import numpy as np
from jax import lax

D = 2048
SPLIT = 4
TOPK = 2
STEPS = 4
BLOCK = 16
ROWS = 64
FHD = 256
EXPERTS = 8
CAP = 32
PIECES = 32
ROWS_ALL = 1024


def block_levels(key, dims, shards, least, top_value):
    level = 1.0
    for dim, blocks in shards:
        draws = jax.random.uniform(jax.random.fold_in(jax.random.fold_in(key, 6), dim), (blocks,), jnp.float32, least / len(shards), top_value / len(shards))
        level = level * jnp.repeat(jnp.exp(draws), dims[dim] // blocks).reshape((-1,) + (1,) * (len(dims) - 1 - dim))
    return level


def shared_out(own_key, own, number, rows, number_of, top, limit, slope):
    ranking = jax.random.permutation(own_key, number_of)
    crowded, usual = shares(number_of, rows * top, limit, slope, True), shares(number_of, rows * top, limit, slope, False)
    places = jnp.arange(number_of)

    def named(lengths, rotation):
        used = int((lengths > 0).sum())
        fixed = max(1, used // 4)
        shifted = fixed + (places - fixed + rotation * (used - fixed)) % max(1, number_of - fixed)
        return jnp.zeros((number_of,), jnp.int32).at[ranking[jnp.where(places < fixed, places, shifted)]].set(jnp.asarray(lengths, jnp.int32))

    lengths = jnp.where(number % 4 == 0, named(crowded, number // 4), named(usual, number - number // 4 - 1))
    mixed = jax.random.permutation(jax.random.fold_in(own, 3), number_of)
    donor, taker = mixed[0:number_of // 2 * 2:2], mixed[1:number_of // 2 * 2:2]
    slack = jnp.minimum(lengths[donor] - 1, limit - lengths[taker]) // 2
    slack = jnp.where((donor == ranking[0]) | (taker == ranking[0]) | (lengths[taker] == 0), 0, jnp.maximum(slack, 0))
    shifted = jax.random.randint(jax.random.fold_in(own, 4), (number_of // 2,), 0, 1 << 20) % (slack + 1)
    lengths = lengths.at[donor].add(-shifted).at[taker].add(shifted)
    labels = jnp.searchsorted(jnp.cumsum(lengths), jnp.arange(rows * top), side="right").astype(jnp.int32)
    grid = labels.reshape(top, rows).T
    grid = grid[jax.random.permutation(jax.random.fold_in(own, 1), rows)]
    rotation = jax.random.randint(jax.random.fold_in(own, 2), (rows, 1), 0, top)
    return jnp.take_along_axis(grid, (jnp.arange(top)[None, :] + rotation) % top, axis=1)


def shares(count, total, limit, skew, full):
    portions = [(1 << 20) // math.isqrt(rank ** skew) + 1 for rank in range(1, count + 1)]
    largest = limit if full else min(limit, max(-(-total // count), total * portions[0] // sum(portions)))
    least = 1 if total - largest >= count - 1 else 0
    holding, surplus = [largest] + [least] * (count - 1), total - largest - least * (count - 1)
    while surplus > 0:
        movable = [i for i in range(1, count) if holding[i] < largest] or [i for i in range(1, count) if holding[i] < limit]
        mass, budget = sum([portions[i] for i in movable]), surplus
        for i in movable:
            more = min(limit - holding[i], max(1, budget * portions[i] // mass), surplus)
            holding[i] = holding[i] + more
            surplus = surplus - more
    return np.array(holding)


def centred(stream_key, shape, deviation, most, pieces=(), kind=jnp.bfloat16):
    result = deviation * jax.random.normal(stream_key, shape, jnp.float32)
    if pieces:
        result = result * block_levels(stream_key, shape, pieces, -0.22, 0.18)
    return jnp.clip(result, -most, most).astype(kind)


def setup_inputs(seed: int = 0) -> dict:
    splits = jax.random.split(jax.random.key(seed), 9)
    tokens = centred(splits[0], (STEPS, ROWS_ALL, D), 1.0, 6.0, ((1, 16), (2, 32)))
    norm_gain = jnp.clip(jnp.exp(jax.random.uniform(splits[1], (D,), jnp.float32, math.log(0.5), math.log(2.0))), 0.5, 2.0).astype(jnp.bfloat16)
    router = centred(splits[2], (D, EXPERTS), D ** -0.5, 0.125)
    routes_keys = jax.random.split(jax.random.fold_in(splits[3], 1), STEPS * ROWS_ALL // ROWS)
    routes_turns = jax.random.permutation(jax.random.fold_in(splits[3], 3), STEPS * ROWS_ALL // ROWS)
    routes = jax.vmap(lambda own, number: shared_out(jax.random.fold_in(splits[3], 2), own, number, ROWS, EXPERTS, TOPK, CAP, 1))(routes_keys, routes_turns).reshape((STEPS, ROWS_ALL, TOPK))
    expert_weights = centred(splits[4], (PIECES, D, 3 * FHD), D ** -0.5, 0.125, ((0, 32),))
    codes = jnp.clip(jax.random.uniform(splits[5], (PIECES, D, 3 * FHD), jnp.float32, -6.0, 6.0) * block_levels(splits[5], (PIECES, D, 3 * FHD), ((0, 32), (1, 16)), -0.4, 0.0), -6.0, 6.0).astype(jnp.bfloat16)
    scales = jnp.clip(jnp.exp(math.log(0.019897461) - 2.2979944 * jax.random.uniform(splits[6], (PIECES, D, 3 * FHD // BLOCK), jnp.float32) ** block_levels(splits[6], (PIECES, D, 3 * FHD // BLOCK), ((0, 32), (1, 16)), -0.2, 0.2)), 0.0019989014, 0.019897461).astype(jnp.bfloat16)
    owner_map = jax.random.permutation(splits[7], D).astype(jnp.int32)
    return dict(tokens=tokens, norm_gain=norm_gain, router=router, routes=routes, expert_weights=expert_weights, codes=codes, scales=scales, owner_map=owner_map)


def reference(tokens, norm_gain, router, routes, expert_weights, codes, scales, owner_map):
    width = 3 * FHD
    decoded = (codes.astype(jnp.float32).reshape(PIECES, D, width // BLOCK, BLOCK) * scales.astype(jnp.float32)[..., None]).reshape(PIECES, D, width)
    inverse = jnp.argsort(owner_map).astype(jnp.int32)
    delta = jnp.take(decoded, inverse, axis=1)
    fresh = (expert_weights.astype(jnp.float32) + delta).astype(jnp.bfloat16)
    inputs = tokens.astype(jnp.float32)
    meansq = lax.optimization_barrier(jnp.mean(inputs * inputs, axis=-1, keepdims=True))
    normed = (inputs * lax.rsqrt(meansq + 1e-06) * norm_gain.astype(jnp.float32)).astype(jnp.bfloat16)
    logits = jnp.einsum('srd,de->sre', normed.astype(jnp.float32), router.astype(jnp.float32))
    chosen = jax.nn.sigmoid(jnp.take_along_axis(logits, routes, axis=-1))
    gates = chosen / lax.optimization_barrier(jnp.sum(chosen, axis=-1, keepdims=True))
    normed_wide = normed.astype(jnp.float32)

    def add_piece(total, item):
        weights, index = item
        expert = index // SPLIT
        share = lax.optimization_barrier(jnp.sum(jnp.where(routes == expert, gates, 0.0), axis=-1))
        both = jnp.einsum('srd,df->srf', normed_wide, weights[:, :2 * FHD].astype(jnp.float32))
        hidden = (jax.nn.silu(both[..., :FHD]) * both[..., FHD:] * share[..., None]).astype(jnp.bfloat16)
        part = jnp.einsum('srf,df->srd', hidden.astype(jnp.float32), weights[:, 2 * FHD:].astype(jnp.float32))
        return (total + part.astype(jnp.bfloat16).astype(jnp.float32), None)
    total, unused = lax.scan(add_piece, jnp.zeros(tokens.shape, jnp.float32), (fresh, jnp.arange(PIECES, dtype=jnp.int32)))
    return (inputs + total).astype(jnp.bfloat16)
```

```python
import jax
import jax.numpy as jnp
from jax import lax
from jax.experimental import pallas as pl
from jax.experimental.pallas import tpu as pltpu
from jax.sharding import PartitionSpec as P

MESH = pl.DeviceIdType.MESH
BF = jnp.bfloat16
F32 = jnp.float32
NX, NZ, NY, NT, NE, CAP = 4, 4, 8, 32, 8, 32
D, F = 2048, 256


def mm(a, b, ca=1, cb=0):
    return lax.dot_general(a, b, (((ca,), (cb,)), ((), ())), preferred_element_type=F32)


def iota(shape, dim):
    return lax.broadcasted_iota(jnp.int32, shape, dim)


def kernel(
    tok_ref, gain_ref, router_ref, routes_ref, w_hbm, codes_ref, scales_ref, om_ref, out_ref,
    w, gu, dn, perm, cmat, ctmat, msg, xr, xn, xp, outm, outr, wsem, ss, rs, ts, tr, os, orr,
):
    rep, tp, zl = lax.axis_index("rep"), lax.axis_index("tp"), lax.axis_index("fsdp")
    x, c = rep // 2, rep % 2
    zh, y = tp // NY, tp % NY
    e0 = tp // 4
    xd, xu, x2 = (x + NX - 1) % NX, (x + 1) % NX, (x + 2) % NX

    def peer(kind):
        if kind == "core":
            return {"rep": x * 2 + (1 - c)}
        if kind == "z":
            return {"fsdp": 1 - zl}
        return {"rep": (xu if kind == "up" else xd) * 2 + c}

    def tdev(k):
        return ((zh + k // NY) % NZ) * NY + (y + k % NY) % NY

    bar = pltpu.get_barrier_semaphore()
    for kind in ("core", "z", "up", "down"):
        pl.semaphore_signal(bar, inc=1, device_id=peer(kind), device_id_type=MESH)

    @pl.loop(1, NT)
    def _(k):
        pl.semaphore_signal(bar, inc=1, device_id={"tp": tdev(k)}, device_id_type=MESH)

    wcopy = pltpu.make_async_copy(w_hbm.at[0], w, wsem)
    wcopy.start()

    own = rep * 2 + zl
    spread = (iota((48, 768), 1) // 16 == iota((48, 768), 0)).astype(BF)
    delta = (codes_ref[0].astype(F32) * mm(scales_ref[0], spread)).astype(BF)
    gu[own] = delta[:, :512]
    dn[own] = delta[:, 512:]

    rt = routes_ref[...].reshape(256, 2)
    lane = iota((256, 128), 1)
    hit = ((rt[:, 0:1] == lane) | (rt[:, 1:2] == lane)).astype(F32)
    hitb = hit.astype(BF)
    ra, rb = iota((256, 256), 0), iota((256, 256), 1)
    before = ((rb < ra) & (ra // 64 == rb // 64)).astype(BF)
    pos = mm(before, hitb)
    expand = (iota((128, 256), 0) == iota((128, 256), 1) // CAP).astype(BF)
    hitx = mm(hitb, expand)
    posx = mm(pos.astype(BF), expand)
    ct = jnp.where(posx == (rb % CAP).astype(F32), hitx, 0.0)
    ctmat[...] = ct.astype(BF)
    cm = ct.T.astype(BF)
    cmat[...] = cm
    tok = tok_ref[...].reshape(256, 64)
    tok2 = jnp.concatenate([tok, tok], axis=1)
    want = iota((256, 128), 0) // 64
    half = lane // 64
    for j in range(2):
        placed = jnp.where(want == 2 * j + half, tok2.astype(F32), 0.0).astype(BF)
        msg[:, j] = mm(cm, placed).astype(BF).reshape(NE, CAP, 128)

    pl.semaphore_wait(bar, 35)

    bufs = (gu, dn)
    sent = []

    def shard(xx, cc, zz):
        return (xx * 2 + cc) * 2 + zz

    def send(part, o, h, kind):
        ref = bufs[part].at[o] if h is None else bufs[part].at[o, pl.ds(64 * h, 64)]
        cp = pltpu.make_async_remote_copy(
            src_ref=ref, dst_ref=ref, send_sem=ss.at[len(sent)],
            recv_sem=rs.at[part, o, 0 if h is None else h],
            device_id=peer(kind), device_id_type=MESH,
        )
        cp.start()
        sent.append(cp)

    def recv(part, o, h):
        ref = bufs[part].at[o] if h is None else bufs[part].at[o, pl.ds(64 * h, 64)]
        pltpu.make_async_remote_copy(
            src_ref=ref, dst_ref=ref, send_sem=ss.at[0],
            recv_sem=rs.at[part, o, 0 if h is None else h],
            device_id=peer("core"), device_id_type=MESH,
        ).wait_recv()

    def first(part):
        send(part, own, 0, "z")
        send(part, own, 0, "up")
        send(part, own, 1, "down")
        send(part, own, 1, "z")
        send(part, own, 1, "up")
        send(part, own, 0, "down")
        send(part, own, None, "core")

    def second(part):
        o = shard(x, c, 1 - zl)
        recv(part, o, 0)
        send(part, o, 0, "up")
        recv(part, o, 1)
        send(part, o, 1, "down")
        send(part, o, 1, "up")
        send(part, o, 0, "down")
        send(part, o, None, "core")

    def third(part, zz):
        lo, hi = shard(xd, c, zz), shard(xu, c, zz)
        recv(part, lo, 0)
        send(part, lo, 0, "up")
        recv(part, hi, 1)
        send(part, hi, 1, "down")
        recv(part, lo, 1)
        send(part, lo, None, "core")
        recv(part, hi, 0)
        send(part, hi, None, "core")

    def fourth(part, zz):
        o = shard(x2, c, zz)
        recv(part, o, 0)
        recv(part, o, 1)
        send(part, o, None, "core")

    def fifth(part):
        for xx in range(NX):
            for zz in range(2):
                recv(part, shard(xx, 1 - c, zz), None)

    first(0)

    def tcopy(k):
        t = tdev(k)
        return pltpu.make_async_remote_copy(
            src_ref=msg.at[t // 4], dst_ref=xr.at[tp], send_sem=ts.at[k], recv_sem=tr.at[tp],
            device_id={"tp": t}, device_id_type=MESH,
        )

    def twait(k):
        t = tdev(k)
        return pltpu.make_async_remote_copy(
            src_ref=msg.at[0], dst_ref=xr.at[t], send_sem=ts.at[k], recv_sem=tr.at[t],
            device_id={"tp": t}, device_id_type=MESH,
        )

    @pl.loop(1, NT)
    def _(k):
        tcopy(k).start()

    xr[tp] = msg[e0]

    def build(lo, hi):
        @pl.loop(lo, hi)
        def _(i):
            base = pl.multiple_of(i * 128, 128)
            perm[pl.ds(base, 128), :] = jnp.where(
                iota((128, D), 0) + base == om_ref[...], 1.0, 0.0
            ).astype(BF)

    build(0, 8)
    second(0)
    build(8, 16)
    third(0, zl)
    first(1)
    third(0, 1 - zl)

    @pl.loop(1, NT)
    def _(k):
        twait(k).wait_recv()

    low = iota((64, 128), 1) < 64
    for u in range(NT // 2):
        a = xr[2 * u].reshape(64, 128).astype(F32)
        b = xr[2 * u + 1].reshape(64, 128).astype(F32)
        xn[:64, 128 * u : 128 * u + 128] = jnp.where(low, a, pltpu.roll(b, 64, 1)).astype(BF)
        xn[64:, 128 * u : 128 * u + 128] = jnp.where(low, pltpu.roll(a, 64, 1), b).astype(BF)
    rows = xn[...].astype(F32)
    scale = lax.rsqrt(jnp.mean(rows * rows, axis=-1, keepdims=True) + 1e-06)
    xn[...] = (rows * scale * gain_ref[...].astype(F32)).astype(BF)

    second(1)
    fourth(0, zl)
    fourth(0, 1 - zl)

    logits = mm(xn[...], router_ref[...])
    mine = cmat[pl.ds(pl.multiple_of(e0 * CAP, CAP), CAP), :].astype(F32)
    four = jnp.concatenate([mine, mine, mine, mine], axis=0)
    rowid = iota((128, 256), 0)
    step = (rowid // 32 % 2) * 2 + rowid // 64
    chosen = mm(jnp.where(iota((128, 256), 1) // 64 == step, four, 0.0).astype(BF), hitb)[:, :NE]
    sig = jax.nn.sigmoid(logits) * chosen
    total = jnp.sum(sig, axis=-1, keepdims=True)
    this = jnp.sum(jnp.where(iota((128, NE), 1) == e0, sig, 0.0), axis=-1, keepdims=True)
    used = jnp.sum(chosen, axis=-1, keepdims=True) > 0.5
    share = jnp.where(used, this / jnp.where(used, total, 1.0), 0.0)

    @pl.loop(0, 8)
    def _(i):
        at = pl.ds(pl.multiple_of(i * 256, 256), 256)
        xp[:, at] = mm(xn[...], perm[:, at]).astype(BF)

    third(1, zl)
    third(1, 1 - zl)
    wcopy.wait()
    both = mm(xn[...], w[:, : 2 * F])
    fifth(0)
    both = both + mm(xp[...], gu[...].reshape(D, 2 * F))
    hidden = (jax.nn.silu(both[:, :F]) * both[:, F:] * share).astype(BF)
    fourth(1, zl)
    fourth(1, 1 - zl)
    fifth(1)
    xp[...] = mm(hidden, dn[...].reshape(D, F), 1, 1).astype(BF)

    def odest(k):
        return ((tp // 4 + k // 4) % NE) * 4 + (tp % 4 + k % 4) % 4

    def ocopy(k):
        t = odest(k)
        return pltpu.make_async_remote_copy(
            src_ref=outm.at[t], dst_ref=outr.at[tp % 4, tp // 4], send_sem=os.at[k],
            recv_sem=orr.at[tp], device_id={"tp": t}, device_id_type=MESH,
        )

    def owait(k):
        t = odest(k)
        return pltpu.make_async_remote_copy(
            src_ref=outm.at[t], dst_ref=outr.at[t % 4, t // 4], send_sem=os.at[k],
            recv_sem=orr.at[t], device_id={"tp": t}, device_id_type=MESH,
        )

    @pl.loop(0, 8)
    def _(i):
        g = (tp // 4 + i) % NE
        at = pl.ds(pl.multiple_of(g * 256, 256), 256)
        part = mm(hidden, w[at, 2 * F :], 1, 1) + mm(xp[...], perm[at, :], 1, 1)
        for u in range(2):
            even, odd = part[:64, 128 * u : 128 * u + 128], part[64:, 128 * u : 128 * u + 128]
            outm[g * 4 + 2 * u] = jnp.where(low, even, pltpu.roll(odd, 64, 1)).astype(BF).reshape(2, CAP, 128)
            outm[g * 4 + 2 * u + 1] = jnp.where(low, pltpu.roll(even, 64, 1), odd).astype(BF).reshape(2, CAP, 128)

        @pl.when(i > 0)
        def _():
            ocopy(4 * i).start()

        for q in range(1, 4):
            ocopy(4 * i + q).start()

    outr[tp % 4, tp // 4] = outm[tp]

    for cp in sent:
        cp.wait_send()

    @pl.loop(1, NT)
    def _(k):
        tcopy(k).wait_send()
        owait(k).wait_recv()

    for j in range(2):
        acc = jnp.zeros((128, 128), F32)
        for q in range(4):
            acc = acc + mm(ctmat[128 * j : 128 * j + 128, :], outr[q, :, j].reshape(256, 128))
        for a in range(2):
            s = 2 * j + a
            out_ref[s] = (
                tok_ref[s].astype(F32) + acc[64 * a : 64 * a + 64, 64 * a : 64 * a + 64]
            ).astype(BF)

    @pl.loop(1, NT)
    def _(k):
        ocopy(k).wait_send()


def body(tokens, norm_gain, router, routes, expert_weights, codes, scales, owner_map):
    vm = pl.BlockSpec(memory_space=pltpu.VMEM)
    dma = pltpu.SemaphoreType.DMA
    return pl.pallas_call(
        kernel,
        out_shape=jax.ShapeDtypeStruct(tokens.shape, BF),
        in_specs=[vm, vm, vm, vm, pl.BlockSpec(memory_space=pl.ANY), vm, vm, vm],
        out_specs=vm,
        scratch_shapes=[
            pltpu.VMEM((D, 3 * F), BF),
            pltpu.VMEM((16, 128, 2 * F), BF),
            pltpu.VMEM((16, 128, F), BF),
            pltpu.VMEM((D, D), BF),
            pltpu.VMEM((256, 256), BF),
            pltpu.VMEM((256, 256), BF),
            pltpu.VMEM((NE, 2, CAP, 128), BF),
            pltpu.VMEM((NT, 2, CAP, 128), BF),
            pltpu.VMEM((128, D), BF),
            pltpu.VMEM((128, D), BF),
            pltpu.VMEM((NT, 2, CAP, 128), BF),
            pltpu.VMEM((4, NE, 2, CAP, 128), BF),
            dma, dma((48,)), dma((2, 16, 2)),
            dma((NT,)), dma((NT,)), dma((NT,)), dma((NT,)),
        ],
        compiler_params=pltpu.CompilerParams(
            collective_id=0, has_side_effects=True, vmem_limit_bytes=48 << 20
        ),
        cost_estimate=pl.CostEstimate(flops=4 * 10**9, bytes_accessed=8 << 20, transcendentals=0),
    )(
        tokens, norm_gain.reshape(1, D), router, routes, expert_weights, codes, scales,
        owner_map.reshape(1, D),
    )


def solution(mesh):
    placed = (
        P(None, ("rep", "fsdp"), "tp"),
        P(),
        P(),
        P(None, ("rep", "fsdp"), None),
        P("tp", None, None),
        P("tp", ("rep", "fsdp"), None),
        P("tp", ("rep", "fsdp"), None),
        P(),
    )
    return jax.shard_map(
        body, mesh=mesh, in_specs=placed, out_specs=P(None, ("rep", "fsdp"), "tp"), check_vma=False
    )
```

```python
import jax
import jax.numpy as jnp
from jax import lax
from jax.experimental import pallas as pl
from jax.experimental.pallas import tpu as pltpu
from jax.sharding import PartitionSpec as P

MESH = pl.DeviceIdType.MESH
BF = jnp.bfloat16
F32 = jnp.float32
NX, NZ, NY, NT, NE, CAP = 4, 4, 8, 32, 8, 32
D, F = 2048, 256


def mm(a, b, ca=1, cb=0):
    return lax.dot_general(a, b, (((ca,), (cb,)), ((), ())), preferred_element_type=F32)


def iota(shape, dim):
    return lax.broadcasted_iota(jnp.int32, shape, dim)


def kernel(
    tok_hbm, gain_hbm, router_hbm, routes_hbm, w_hbm, codes_hbm, scales_hbm, om_hbm, out_ref,
    tok_ref, gain_ref, router_ref, routes_ref, codes_ref, scales_ref, om_ref, grow, w, gu, dn, perm, cmat, ctmat, msg, xr, xn, xp, outm, outr, wsem, ss, rs, ts, tr, os, orr,
):
    rep, tp, zl = lax.axis_index("rep"), lax.axis_index("tp"), lax.axis_index("fsdp")
    x, c = rep // 2, rep % 2
    zh, y = tp // NY, tp % NY
    e0 = tp // 4
    xd, xu, x2 = (x + NX - 1) % NX, (x + 1) % NX, (x + 2) % NX

    def peer(kind):
        if kind == "core":
            return {"rep": x * 2 + (1 - c)}
        if kind == "z":
            return {"fsdp": 1 - zl}
        return {"rep": (xu if kind == "up" else xd) * 2 + c}

    def tdev(k):
        return ((zh + k // NY) % NZ) * NY + (y + k % NY) % NY

    bar = pltpu.get_barrier_semaphore()
    for kind in ("core", "z", "up", "down"):
        pl.semaphore_signal(bar, inc=1, device_id=peer(kind), device_id_type=MESH)

    @pl.loop(1, NT)
    def _(k):
        pl.semaphore_signal(bar, inc=1, device_id={"tp": tdev(k)}, device_id_type=MESH)

    pairs = (
        (codes_hbm.at[0], codes_ref), (scales_hbm.at[0], scales_ref), (routes_hbm, routes_ref),
        (tok_hbm, tok_ref), (om_hbm, om_ref), (router_hbm, router_ref), (gain_hbm, gain_ref),
        (w_hbm.at[0], w),
    )
    loads = [pltpu.make_async_copy(a, b, wsem.at[i]) for i, (a, b) in enumerate(pairs)]
    for cp in loads:
        cp.start()
    loads[0].wait()
    loads[1].wait()

    own = rep * 2 + zl
    spread = (iota((48, 768), 1) // 16 == iota((48, 768), 0)).astype(BF)
    delta = (codes_ref[...].astype(F32) * mm(scales_ref[...], spread, 0, 0)).astype(BF)
    gu[own] = delta[:, :512]
    dn[own] = delta[:, 512:]

    loads[2].wait()
    loads[3].wait()
    lane = iota((256, 128), 1)
    name = iota((128, 64), 0)
    hit = jnp.concatenate(
        [
            ((routes_ref[s, 0:1, :] == name) | (routes_ref[s, 1:2, :] == name)).astype(F32).T
            for s in range(4)
        ],
        axis=0,
    )
    hitb = hit.astype(BF)
    ra, rb = iota((256, 256), 0), iota((256, 256), 1)
    before = ((rb < ra) & (ra // 64 == rb // 64)).astype(BF)
    pos = mm(before, hitb)
    expand = (iota((128, 256), 0) == iota((128, 256), 1) // CAP).astype(BF)
    hitx = mm(hitb, expand)
    posx = mm(pos.astype(BF), expand)
    ct = jnp.where(posx == (rb % CAP).astype(F32), hitx, 0.0)
    ctmat[...] = ct.astype(BF)
    cm = ct.T.astype(BF)
    cmat[...] = cm
    tok = tok_ref[...].reshape(256, 64)
    tok2 = jnp.concatenate([tok, tok], axis=1)
    want = iota((256, 128), 0) // 64
    half = lane // 64
    for j in range(2):
        placed = jnp.where(want == 2 * j + half, tok2.astype(F32), 0.0).astype(BF)
        msg[:, j] = mm(cm, placed).astype(BF).reshape(NE, CAP, 128)

    pl.semaphore_wait(bar, 35)

    bufs = (gu, dn)
    sent = []

    def shard(xx, cc, zz):
        return (xx * 2 + cc) * 2 + zz

    def send(part, o, h, kind):
        ref = bufs[part].at[o] if h is None else bufs[part].at[o, pl.ds(64 * h, 64)]
        cp = pltpu.make_async_remote_copy(
            src_ref=ref, dst_ref=ref, send_sem=ss.at[len(sent)],
            recv_sem=rs.at[part, o, 0 if h is None else h],
            device_id=peer(kind), device_id_type=MESH,
        )
        cp.start()
        sent.append(cp)

    def recv(part, o, h):
        ref = bufs[part].at[o] if h is None else bufs[part].at[o, pl.ds(64 * h, 64)]
        pltpu.make_async_remote_copy(
            src_ref=ref, dst_ref=ref, send_sem=ss.at[0],
            recv_sem=rs.at[part, o, 0 if h is None else h],
            device_id=peer("core"), device_id_type=MESH,
        ).wait_recv()

    def first(part):
        send(part, own, 0, "z")
        send(part, own, 0, "up")
        send(part, own, 1, "down")
        send(part, own, 1, "z")
        send(part, own, 1, "up")
        send(part, own, 0, "down")
        send(part, own, None, "core")

    def second(part):
        o = shard(x, c, 1 - zl)
        recv(part, o, 0)
        send(part, o, 0, "up")
        recv(part, o, 1)
        send(part, o, 1, "down")
        send(part, o, 1, "up")
        send(part, o, 0, "down")
        send(part, o, None, "core")

    def third(part, zz):
        lo, hi = shard(xd, c, zz), shard(xu, c, zz)
        recv(part, lo, 0)
        send(part, lo, 0, "up")
        recv(part, hi, 1)
        send(part, hi, 1, "down")
        recv(part, lo, 1)
        send(part, lo, None, "core")
        recv(part, hi, 0)
        send(part, hi, None, "core")

    def fourth(part, zz):
        o = shard(x2, c, zz)
        recv(part, o, 0)
        recv(part, o, 1)
        send(part, o, None, "core")

    def fifth(part):
        for xx in range(NX):
            for zz in range(2):
                recv(part, shard(xx, 1 - c, zz), None)

    first(0)
    for cp in loads[4:7]:
        cp.wait()

    def tcopy(k):
        t = tdev(k)
        return pltpu.make_async_remote_copy(
            src_ref=msg.at[t // 4], dst_ref=xr.at[tp], send_sem=ts.at[k], recv_sem=tr.at[tp],
            device_id={"tp": t}, device_id_type=MESH,
        )

    def twait(k):
        t = tdev(k)
        return pltpu.make_async_remote_copy(
            src_ref=msg.at[0], dst_ref=xr.at[t], send_sem=ts.at[k], recv_sem=tr.at[t],
            device_id={"tp": t}, device_id_type=MESH,
        )

    @pl.loop(1, NT)
    def _(k):
        tcopy(k).start()

    xr[tp] = msg[e0]

    def build(lo, hi):
        @pl.loop(lo, hi)
        def _(i):
            base = pl.multiple_of(i * 128, 128)
            perm[pl.ds(base, 128), :] = jnp.where(
                iota((128, D), 0) + base == om_ref[...], 1.0, 0.0
            ).astype(BF)

    build(0, 8)
    second(0)
    build(8, 16)
    third(0, zl)
    first(1)
    third(0, 1 - zl)

    @pl.loop(1, NT)
    def _(k):
        twait(k).wait_recv()

    low = iota((64, 128), 1) < 64
    for u in range(NT // 2):
        a = xr[2 * u].reshape(64, 128).astype(F32)
        b = xr[2 * u + 1].reshape(64, 128).astype(F32)
        xn[:64, 128 * u : 128 * u + 128] = jnp.where(low, a, pltpu.roll(b, 64, 1)).astype(BF)
        xn[64:, 128 * u : 128 * u + 128] = jnp.where(low, pltpu.roll(a, 64, 1), b).astype(BF)
    for u in range(16):
        grow[:, 128 * u : 128 * u + 128] = gain_ref[u : u + 1, :].astype(F32)
    rows = xn[...].astype(F32)
    scale = lax.rsqrt(jnp.mean(rows * rows, axis=-1, keepdims=True) + 1e-06)
    xn[...] = (rows * scale * grow[...]).astype(BF)

    second(1)
    fourth(0, zl)
    fourth(0, 1 - zl)

    logits = mm(xn[...], router_ref[...], 1, 1)
    mine = cmat[pl.ds(pl.multiple_of(e0 * CAP, CAP), CAP), :].astype(F32)
    four = jnp.concatenate([mine, mine, mine, mine], axis=0)
    rowid = iota((128, 256), 0)
    step = (rowid // 32 % 2) * 2 + rowid // 64
    chosen = mm(jnp.where(iota((128, 256), 1) // 64 == step, four, 0.0).astype(BF), hitb)[:, :NE]
    sig = jax.nn.sigmoid(logits) * chosen
    total = jnp.sum(sig, axis=-1, keepdims=True)
    this = jnp.sum(jnp.where(iota((128, NE), 1) == e0, sig, 0.0), axis=-1, keepdims=True)
    used = jnp.sum(chosen, axis=-1, keepdims=True) > 0.5
    share = jnp.where(used, this / jnp.where(used, total, 1.0), 0.0)

    @pl.loop(0, 8)
    def _(i):
        at = pl.ds(pl.multiple_of(i * 256, 256), 256)
        xp[:, at] = mm(xn[...], perm[:, at]).astype(BF)

    third(1, zl)
    third(1, 1 - zl)
    loads[7].wait()
    both = mm(xn[...], w[:, : 2 * F])
    fifth(0)
    both = both + mm(xp[...], gu[...].reshape(D, 2 * F))
    hidden = (jax.nn.silu(both[:, :F]) * both[:, F:] * share).astype(BF)
    fourth(1, zl)
    fourth(1, 1 - zl)
    fifth(1)
    xp[...] = mm(hidden, dn[...].reshape(D, F), 1, 1).astype(BF)

    def odest(k):
        return ((tp // 4 + k // 4) % NE) * 4 + (tp % 4 + k % 4) % 4

    def ocopy(k):
        t = odest(k)
        return pltpu.make_async_remote_copy(
            src_ref=outm.at[t], dst_ref=outr.at[tp % 4, tp // 4], send_sem=os.at[k],
            recv_sem=orr.at[tp], device_id={"tp": t}, device_id_type=MESH,
        )

    def owait(k):
        t = odest(k)
        return pltpu.make_async_remote_copy(
            src_ref=outm.at[t], dst_ref=outr.at[t % 4, t // 4], send_sem=os.at[k],
            recv_sem=orr.at[t], device_id={"tp": t}, device_id_type=MESH,
        )

    @pl.loop(0, 8)
    def _(i):
        g = (tp // 4 + i) % NE
        at = pl.ds(pl.multiple_of(g * 256, 256), 256)
        part = mm(hidden, w[at, 2 * F :], 1, 1) + mm(xp[...], perm[at, :], 1, 1)
        for u in range(2):
            even, odd = part[:64, 128 * u : 128 * u + 128], part[64:, 128 * u : 128 * u + 128]
            outm[g * 4 + 2 * u] = jnp.where(low, even, pltpu.roll(odd, 64, 1)).astype(BF).reshape(2, CAP, 128)
            outm[g * 4 + 2 * u + 1] = jnp.where(low, pltpu.roll(even, 64, 1), odd).astype(BF).reshape(2, CAP, 128)

        @pl.when(i > 0)
        def _():
            ocopy(4 * i).start()

        for q in range(1, 4):
            ocopy(4 * i + q).start()

    outr[tp % 4, tp // 4] = outm[tp]

    for cp in sent:
        cp.wait_send()

    @pl.loop(1, NT)
    def _(k):
        tcopy(k).wait_send()
        owait(k).wait_recv()

    for j in range(2):
        acc = jnp.zeros((128, 128), F32)
        for q in range(4):
            acc = acc + mm(ctmat[128 * j : 128 * j + 128, :], outr[q, :, j].reshape(256, 128))
        for a in range(2):
            s = 2 * j + a
            out_ref[s] = (
                tok_ref[s].astype(F32) + acc[64 * a : 64 * a + 64, 64 * a : 64 * a + 64]
            ).astype(BF)

    @pl.loop(1, NT)
    def _(k):
        ocopy(k).wait_send()


def body(tokens, norm_gain, router, routes, expert_weights, codes, scales, owner_map):
    vm = pl.BlockSpec(memory_space=pltpu.VMEM)
    dma = pltpu.SemaphoreType.DMA
    return pl.pallas_call(
        kernel,
        out_shape=jax.ShapeDtypeStruct(tokens.shape, BF),
        in_specs=[pl.BlockSpec(memory_space=pltpu.HBM)] * 8,
        out_specs=vm,
        scratch_shapes=[
            pltpu.VMEM((4, 64, 64), BF),
            pltpu.VMEM((16, 128), BF),
            pltpu.VMEM((NE, D), BF),
            pltpu.VMEM((4, 2, 64), jnp.int32),
            pltpu.VMEM((128, 3 * F), BF),
            pltpu.VMEM((48, 128), BF),
            pltpu.VMEM((1, D), jnp.int32),
            pltpu.VMEM((1, D), F32),
            pltpu.VMEM((D, 3 * F), BF),
            pltpu.VMEM((16, 128, 2 * F), BF),
            pltpu.VMEM((16, 128, F), BF),
            pltpu.VMEM((D, D), BF),
            pltpu.VMEM((256, 256), BF),
            pltpu.VMEM((256, 256), BF),
            pltpu.VMEM((NE, 2, CAP, 128), BF),
            pltpu.VMEM((NT, 2, CAP, 128), BF),
            pltpu.VMEM((128, D), BF),
            pltpu.VMEM((128, D), BF),
            pltpu.VMEM((NT, 2, CAP, 128), BF),
            pltpu.VMEM((4, NE, 2, CAP, 128), BF),
            dma((8,)), dma((48,)), dma((2, 16, 2)),
            dma((NT,)), dma((NT,)), dma((NT,)), dma((NT,)),
        ],
        compiler_params=pltpu.CompilerParams(
            collective_id=0, has_side_effects=True, vmem_limit_bytes=60 << 20
        ),
        cost_estimate=pl.CostEstimate(flops=4 * 10**9, bytes_accessed=8 << 20, transcendentals=0),
    )(
        tokens, norm_gain.reshape(16, 128), router.T, routes.transpose(0, 2, 1), expert_weights,
        codes, scales.transpose(0, 2, 1), owner_map.reshape(1, D),
    )


def solution(mesh):
    placed = (
        P(None, ("rep", "fsdp"), "tp"),
        P(),
        P(),
        P(None, ("rep", "fsdp"), None),
        P("tp", None, None),
        P("tp", ("rep", "fsdp"), None),
        P("tp", ("rep", "fsdp"), None),
        P(),
    )
    return jax.shard_map(
        body, mesh=mesh, in_specs=placed, out_specs=P(None, ("rep", "fsdp"), "tp"), check_vma=False
    )
```

```python
import jax
import jax.numpy as jnp
from jax import lax
from jax.experimental import pallas as pl
from jax.experimental.pallas import tpu as pltpu
from jax.sharding import PartitionSpec as P

MESH = pl.DeviceIdType.MESH
BF = jnp.bfloat16
F32 = jnp.float32
NX, NZ, NY, NE, CAP = 4, 4, 8, 8, 32
D, F = 2048, 256
ZB = D // NZ


def mm(a, b, ca=1, cb=0):
    return lax.dot_general(a, b, (((ca,), (cb,)), ((), ())), preferred_element_type=F32)


def iota(shape, dim):
    return lax.broadcasted_iota(jnp.int32, shape, dim)


def kernel(
    tok_hbm, gain_hbm, router_hbm, routes_hbm, w_hbm, codes_hbm, scales_hbm, om_hbm, out_ref,
    tok_ref, gain_ref, router_ref, routes_ref, codes_ref, scales_ref, om_ref, grow, omrow,
    w, gu, dn, perm, cmat, ctmat, msg, zm, xr, xg, xacc, xp, outm, outr, zs, zr,
    wsem, dsend, drecv, dcore, zsend, zrecv, ysend, yrecv, osend, orecv, psend, precv,
):
    rep, tp, zl = lax.axis_index("rep"), lax.axis_index("tp"), lax.axis_index("fsdp")
    x, c = rep // 2, rep % 2
    zh, y = tp // NY, tp % NY
    e0 = tp // 4
    x1, x2, x3 = (x + 1) % NX, (x + 2) % NX, (x + 3) % NX

    def peer(kind):
        if kind == "core":
            return {"rep": x * 2 + (1 - c)}
        if kind == "z":
            return {"fsdp": 1 - zl}
        return {"rep": (x1 if kind == "up" else x3) * 2 + c}

    def ydev(r):
        return {"tp": zh * NY + (y + r) % NY}

    def zdev(r):
        return {"tp": ((zh + r) % NZ) * NY + y}

    def remote(src, dst, ssem, rsem, dev):
        return pltpu.make_async_remote_copy(
            src_ref=src, dst_ref=dst, send_sem=ssem, recv_sem=rsem, device_id=dev,
            device_id_type=MESH,
        )

    bar = pltpu.get_barrier_semaphore()
    partners = [peer(k) for k in ("core", "z", "up", "down")]
    partners += [ydev(r) for r in range(1, NY)] + [zdev(r) for r in range(1, NZ)]
    for dev in partners:
        pl.semaphore_signal(bar, inc=1, device_id=dev, device_id_type=MESH)

    pairs = (
        (codes_hbm.at[0], codes_ref), (scales_hbm.at[0], scales_ref), (routes_hbm, routes_ref),
        (tok_hbm, tok_ref), (om_hbm, om_ref), (router_hbm, router_ref), (gain_hbm, gain_ref),
        (w_hbm.at[0], w),
    )
    loads = [pltpu.make_async_copy(a, b, wsem.at[i]) for i, (a, b) in enumerate(pairs)]
    for cp in loads:
        cp.start()

    loads[0].wait()
    loads[1].wait()

    def block(cc, xx, zz):
        return cc * 8 + xx * 2 + zz

    own = block(c, x, zl)
    spread = (iota((48, 768), 1) // 16 == iota((48, 768), 0)).astype(BF)
    delta = (codes_ref[...].astype(F32) * mm(scales_ref[...], spread, 0, 0)).astype(BF)
    gu[own] = delta[:, : 2 * F]
    dn[own] = delta[:, 2 * F :]

    loads[2].wait()
    loads[3].wait()
    lane = iota((256, 128), 1)
    name = iota((128, 64), 0)
    hit = jnp.concatenate(
        [
            ((routes_ref[s, 0:1, :] == name) | (routes_ref[s, 1:2, :] == name)).astype(F32).T
            for s in range(4)
        ],
        axis=0,
    )
    hitb = hit.astype(BF)
    ra, rb = iota((256, 256), 0), iota((256, 256), 1)
    before = ((rb < ra) & (ra // 64 == rb // 64)).astype(BF)
    pos = mm(before, hitb)
    expand = (iota((128, 256), 0) == iota((128, 256), 1) // CAP).astype(BF)
    hitx = mm(hitb, expand)
    posx = mm(pos.astype(BF), expand)
    ct = jnp.where(posx == (rb % CAP).astype(F32), hitx, 0.0)
    ctmat[...] = ct.astype(BF)
    cm = ct.T.astype(BF)
    cmat[...] = cm
    tok = tok_ref[...].reshape(256, 64)
    tok2 = jnp.concatenate([tok, tok], axis=1)
    want = iota((256, 128), 0) // 64
    half = lane // 64
    for j in range(2):
        placed = jnp.where(want == 2 * j + half, tok2.astype(F32), 0.0).astype(BF)
        msg[:, j] = mm(cm, placed).astype(BF).reshape(NE, CAP, 128)

    pl.semaphore_wait(bar, len(partners))

    bufs = (gu, dn)

    def send(part, o, h, kind):
        ref = bufs[part].at[o] if h is None else bufs[part].at[o, pl.ds(64 * h, 64)]
        sem = dcore.at[part] if kind == "core" else drecv.at[part, o, 0 if h is None else h]
        remote(ref, ref, dsend.at[part], sem, peer(kind)).start()

    def recv(part, o, h):
        ref = bufs[part].at[o] if h is None else bufs[part].at[o, pl.ds(64 * h, 64)]
        sem = drecv.at[part, o, 0 if h is None else h]
        remote(ref, ref, dsend.at[part], sem, peer("core")).wait_recv()

    def spread_x(part, o):
        send(part, o, 0, "up")
        send(part, o, 1, "down")
        send(part, o, 1, "up")
        send(part, o, 0, "down")

    def first(part):
        send(part, own, None, "z")
        spread_x(part, own)
        send(part, own, None, "core")

    def second(part):
        o = block(c, x, 1 - zl)
        recv(part, o, None)
        spread_x(part, o)
        send(part, o, None, "core")

    def third(part, zz):
        lo, hi = block(c, x3, zz), block(c, x1, zz)
        recv(part, lo, 0)
        send(part, lo, 0, "up")
        recv(part, hi, 1)
        send(part, hi, 1, "down")
        recv(part, lo, 1)
        send(part, lo, None, "core")
        recv(part, hi, 0)
        send(part, hi, None, "core")

    def fourth(part, zz):
        o = block(c, x2, zz)
        recv(part, o, 0)
        recv(part, o, 1)
        send(part, o, None, "core")

    def fifth(part):
        ref = bufs[part].at[pl.ds(8 * (1 - c), 8)]
        remote(ref, ref, dsend.at[part], dcore.at[part], peer("core")).wait_recv()

    def zcopy(r, src):
        return remote(msg.at[pl.ds(2 * ((zh + r) % NZ), 2)], zm.at[src], zsend.at[r], zrecv.at[src], zdev(r))

    def zget(r):
        src = (zh + r) % NZ
        zcopy(r, src).wait_recv()
        yput(src)

    def yput(src):
        for r in range(1, NY):
            to = (y + r) % NY
            remote(zm.at[src, to // 4], xr.at[src, y], ysend.at[src], yrecv.at[src], ydev(r)).start()
        pltpu.make_async_copy(zm.at[src, y // 4], xr.at[src, y], yrecv.at[src]).start()

    for r in (1, 3, 2):
        zcopy(r, zh).start()
    zm[zh] = msg[pl.ds(2 * zh, 2)]
    first(0)
    yput(zh)

    for cp in loads[4:7]:
        cp.wait()
    for cc in range(2):
        for xx in range(NX):
            for zz in range(2):
                s = (xx * 2 + cc) * 2 + zz
                b = block(cc, xx, zz)
                omrow[:, 128 * b : 128 * b + 128] = om_ref[:, 128 * s : 128 * s + 128]
    for u in range(16):
        grow[:, 128 * u : 128 * u + 128] = gain_ref[u : u + 1, :].astype(F32)

    def build(lo, hi):
        @pl.loop(lo, hi)
        def _(i):
            base = pl.multiple_of(i * 128, 128)
            perm[pl.ds(base, 128), :] = jnp.where(
                iota((128, D), 0) + base == omrow[...], 1.0, 0.0
            ).astype(BF)

    low = iota((64, 128), 1) < 64

    def quarter(r, carry):
        zz = (zh + r) % NZ
        remote(xr.at[zz], xr.at[zz], ysend.at[zz], yrecv.at[zz], ydev(1)).wait_recv()
        ssq, wacc, lacc = carry
        for u in range(NY // 2):
            a = xr[zz, 2 * u].reshape(64, 128).astype(F32)
            b = xr[zz, 2 * u + 1].reshape(64, 128).astype(F32)
            g = grow[:, pl.ds(pl.multiple_of(zz * ZB + 128 * u, 128), 128)]
            even = jnp.where(low, a, pltpu.roll(b, 64, 1))
            odd = jnp.where(low, pltpu.roll(a, 64, 1), b)
            ssq = ssq + jnp.concatenate([even * even, odd * odd], axis=0)
            xg[:64, 128 * u : 128 * u + 128] = (even * g).astype(BF)
            xg[64:, 128 * u : 128 * u + 128] = (odd * g).astype(BF)
        at = pl.ds(pl.multiple_of(zz * ZB, ZB), ZB)
        wacc = wacc + mm(xg[...], w[at, : 2 * F])
        lacc = lacc + mm(xg[...], router_ref[:, at], 1, 1)

        @pl.loop(0, 4)
        def _(i):
            cols = pl.ds(pl.multiple_of(i * 512, 512), 512)
            got = mm(xg[...], perm[at, cols])
            if r == 0:
                xacc[:, cols] = got
            else:
                xacc[:, cols] += got

        return ssq, wacc, lacc

    build(0, 8)
    zget(1)
    zget(3)
    second(0)
    zget(2)
    first(1)
    build(8, 16)
    third(0, zl)
    second(1)
    loads[7].wait()
    carry = (jnp.zeros((128, 128), F32), jnp.zeros((128, 2 * F), F32), jnp.zeros((128, NE), F32))
    carry = quarter(0, carry)
    third(0, 1 - zl)
    third(1, zl)
    carry = quarter(1, carry)
    fourth(0, zl)
    fourth(0, 1 - zl)
    third(1, 1 - zl)
    carry = quarter(3, carry)
    fourth(1, zl)
    ssq, wacc, lacc = quarter(2, carry)

    scale = lax.rsqrt(jnp.sum(ssq, axis=-1, keepdims=True) * (1.0 / D) + 1e-06)
    mine = cmat[pl.ds(pl.multiple_of(e0 * CAP, CAP), CAP), :].astype(F32)
    four = jnp.concatenate([mine, mine, mine, mine], axis=0)
    rowid = iota((128, 256), 0)
    step = (rowid // 32 % 2) * 2 + rowid // 64
    chosen = mm(jnp.where(iota((128, 256), 1) // 64 == step, four, 0.0).astype(BF), hitb)[:, :NE]
    sig = jax.nn.sigmoid(lacc * scale) * chosen
    total = jnp.sum(sig, axis=-1, keepdims=True)
    this = jnp.sum(jnp.where(iota((128, NE), 1) == e0, sig, 0.0), axis=-1, keepdims=True)
    used = jnp.sum(chosen, axis=-1, keepdims=True) > 0.5
    share = jnp.where(used, this / jnp.where(used, total, 1.0), 0.0)
    xp[...] = xacc[...].astype(BF)

    def halfmm(cc):
        at = pl.ds(pl.multiple_of(cc * (D // 2), D // 2), D // 2)
        return mm(xp[:, at], gu[pl.ds(8 * cc, 8)].reshape(D // 2, 2 * F))

    both = wacc + halfmm(c)
    fifth(0)
    both = (both + halfmm(1 - c)) * scale
    hidden = (jax.nn.silu(both[:, :F]) * both[:, F:] * share).astype(BF)
    fourth(1, 1 - zl)
    fifth(1)
    xp[...] = mm(hidden, dn[...].reshape(D, F), 1, 1).astype(BF)

    for r in (1, 2, 3, 0):
        zz = (zh + r) % NZ
        at = pl.ds(pl.multiple_of(zz * ZB, ZB), ZB)
        part = mm(hidden, w[at, 2 * F :], 1, 1) + mm(xp[...], perm[at, :], 1, 1)
        for u in range(NY // 2):
            even, odd = part[:64, 128 * u : 128 * u + 128], part[64:, 128 * u : 128 * u + 128]
            outm[zz, 2 * u] = jnp.where(low, even, pltpu.roll(odd, 64, 1)).astype(BF).reshape(2, CAP, 128)
            outm[zz, 2 * u + 1] = jnp.where(low, pltpu.roll(even, 64, 1), odd).astype(BF).reshape(2, CAP, 128)
        for k in range(1, NY):
            remote(outm.at[zz, (y + k) % NY], outr.at[zz, y], osend.at[r], orecv.at[zz], ydev(k)).start()
        pltpu.make_async_copy(outm.at[zz, y], outr.at[zz, y], orecv.at[zz]).start()

    def sums(r):
        zz = (zh + r) % NZ
        remote(outr.at[zz], outr.at[zz], osend.at[r], orecv.at[zz], ydev(1)).wait_recv()
        got = outr[zz].astype(F32)
        return jnp.stack([jnp.sum(got[:4], axis=0), jnp.sum(got[4:], axis=0)]).astype(BF)

    def pcopy(r, src):
        return remote(zs.at[r], zr.at[src], psend.at[r], precv.at[src], zdev(r))

    for r in (1, 2, 3):
        zs[r] = sums(r)
        pcopy(r, zh).start()
    zr[zh] = sums(0)
    for r in (1, 2, 3):
        pcopy(r, (zh + r) % NZ).wait_recv()

    for j in range(2):
        acc = mm(ctmat[128 * j : 128 * j + 128, :], zr[:, :, j].reshape(256, 128))
        for a in range(2):
            s = 2 * j + a
            out_ref[s] = (
                tok_ref[s].astype(F32) + acc[64 * a : 64 * a + 64, 64 * a : 64 * a + 64]
            ).astype(BF)

    for r in (1, 2, 3):
        zcopy(r, zh).wait_send()
        pcopy(r, zh).wait_send()
    for part in range(2):
        ref = bufs[part].at[pl.ds(0, 15)]
        remote(ref, ref, dsend.at[part], dcore.at[part], peer("core")).wait_send()
    for r in range(NZ):
        ref = xr.at[r, pl.ds(0, NY - 1)]
        remote(ref, ref, ysend.at[r], yrecv.at[r], ydev(1)).wait_send()
        remote(ref, ref, osend.at[r], orecv.at[r], ydev(1)).wait_send()


def body(tokens, norm_gain, router, routes, expert_weights, codes, scales, owner_map):
    dma = pltpu.SemaphoreType.DMA
    vm = pltpu.VMEM
    return pl.pallas_call(
        kernel,
        out_shape=jax.ShapeDtypeStruct(tokens.shape, BF),
        in_specs=[pl.BlockSpec(memory_space=pltpu.HBM)] * 8,
        out_specs=pl.BlockSpec(memory_space=pltpu.VMEM),
        scratch_shapes=[
            vm((4, 64, 64), BF),
            vm((16, 128), BF),
            vm((NE, D), BF),
            vm((4, 2, 64), jnp.int32),
            vm((128, 3 * F), BF),
            vm((48, 128), BF),
            vm((1, D), jnp.int32),
            vm((1, D), F32),
            vm((1, D), jnp.int32),
            vm((D, 3 * F), BF),
            vm((16, 128, 2 * F), BF),
            vm((16, 128, F), BF),
            vm((D, D), BF),
            vm((256, 256), BF),
            vm((256, 256), BF),
            vm((NE, 2, CAP, 128), BF),
            vm((NZ, 2, 2, CAP, 128), BF),
            vm((NZ, NY, 2, CAP, 128), BF),
            vm((128, ZB), BF),
            vm((128, D), F32),
            vm((128, D), BF),
            vm((NZ, NY, 2, CAP, 128), BF),
            vm((NZ, NY, 2, CAP, 128), BF),
            vm((NZ, 2, 2, CAP, 128), BF),
            vm((NZ, 2, 2, CAP, 128), BF),
            dma((8,)), dma((2,)), dma((2, 16, 2)), dma((2,)),
            dma((NZ,)), dma((NZ,)), dma((NZ,)), dma((NZ,)),
            dma((NZ,)), dma((NZ,)), dma((NZ,)), dma((NZ,)),
        ],
        compiler_params=pltpu.CompilerParams(
            collective_id=0, has_side_effects=True, vmem_limit_bytes=60 << 20
        ),
        cost_estimate=pl.CostEstimate(flops=4 * 10**9, bytes_accessed=8 << 20, transcendentals=0),
    )(
        tokens, norm_gain.reshape(16, 128), router.T, routes.transpose(0, 2, 1), expert_weights,
        codes, scales.transpose(0, 2, 1), owner_map.reshape(1, D),
    )


def solution(mesh):
    placed = (
        P(None, ("rep", "fsdp"), "tp"),
        P(),
        P(),
        P(None, ("rep", "fsdp"), None),
        P("tp", None, None),
        P("tp", ("rep", "fsdp"), None),
        P("tp", ("rep", "fsdp"), None),
        P(),
    )
    return jax.shard_map(
        body, mesh=mesh, in_specs=placed, out_specs=P(None, ("rep", "fsdp"), "tp"), check_vma=False
    )
```

```python
import jax
import jax.numpy as jnp
from jax import lax
from jax.experimental import pallas as pl
from jax.experimental.pallas import tpu as pltpu
from jax.sharding import PartitionSpec as P

MESH = pl.DeviceIdType.MESH
BF = jnp.bfloat16
F32 = jnp.float32
NX, NZ, NY, NE, CAP = 4, 4, 8, 8, 32
D, F = 2048, 256
ZB = D // NZ
FAR = (4, 3, 5, 2, 6, 1, 7)


def mm(a, b, ca=1, cb=0):
    return lax.dot_general(a, b, (((ca,), (cb,)), ((), ())), preferred_element_type=F32)


def iota(shape, dim):
    return lax.broadcasted_iota(jnp.int32, shape, dim)


def kernel(
    tok_hbm, gain_hbm, router_hbm, routes_hbm, w_hbm, codes_hbm, scales_hbm, om_hbm, out_ref,
    tok_ref, gain_ref, router_ref, routes_ref, codes_ref, scales_ref, om_ref, grow, omrow,
    w, gu, dn, perm, ptw, hy, cmat, ctmat, msg, zm, xr, xg, xacc, xp, outm, outr, zs, zr,
    wsem, dsend, drecv, dcore, zsend, zrecv, ysend, yrecv, osend, orecv, psend, precv,
):
    rep, tp, zl = lax.axis_index("rep"), lax.axis_index("tp"), lax.axis_index("fsdp")
    x, c = rep // 2, rep % 2
    zh, y = tp // NY, tp % NY
    e0 = tp // 4
    x1, x2, x3 = (x + 1) % NX, (x + 2) % NX, (x + 3) % NX

    def peer(kind):
        if kind == "core":
            return {"rep": x * 2 + (1 - c)}
        if kind == "z":
            return {"fsdp": 1 - zl}
        return {"rep": (x1 if kind == "up" else x3) * 2 + c}

    def ydev(r):
        return {"tp": zh * NY + (y + r) % NY}

    def zdev(r):
        return {"tp": ((zh + r) % NZ) * NY + y}

    def remote(src, dst, ssem, rsem, dev):
        return pltpu.make_async_remote_copy(
            src_ref=src, dst_ref=dst, send_sem=ssem, recv_sem=rsem, device_id=dev,
            device_id_type=MESH,
        )

    pairs = (
        (scales_hbm.at[0], scales_ref), (codes_hbm.at[0], codes_ref), (routes_hbm, routes_ref),
        (tok_hbm, tok_ref), (om_hbm, om_ref), (router_hbm, router_ref), (gain_hbm, gain_ref),
        (w_hbm.at[0], w),
    )
    loads = [pltpu.make_async_copy(a, b, wsem.at[i]) for i, (a, b) in enumerate(pairs)]
    for cp in loads:
        cp.start()

    bar = pltpu.get_barrier_semaphore()
    partners = [peer(k) for k in ("core", "z", "up", "down")]
    partners += [ydev(r) for r in range(1, NY)] + [zdev(r) for r in range(1, NZ)]
    for dev in partners:
        pl.semaphore_signal(bar, inc=1, device_id=dev, device_id_type=MESH)

    loads[0].wait()
    loads[1].wait()

    def block(cc, xx, zz):
        return cc * 8 + xx * 2 + zz

    def slots(b, n=1):
        return pl.ds(pl.multiple_of(b * 128, 128), n * 128)

    own = block(c, x, zl)
    spread = (iota((48, 768), 1) // 16 == iota((48, 768), 0)).astype(BF)
    delta = codes_ref[...].astype(F32) * mm(scales_ref[...], spread, 0, 0)
    gu[own] = delta[:, : 2 * F].astype(BF)
    dn[:, slots(own)] = delta[:, 2 * F :].T.astype(BF)

    pl.semaphore_wait(bar, len(partners))

    def shard(part, o, h):
        if part == 0:
            return gu.at[o] if h is None else gu.at[o, pl.ds(64 * h, 64)]
        return dn.at[:, slots(o)] if h is None else dn.at[pl.ds(128 * h, 128), slots(o)]

    def send(part, o, h, kind):
        ref = shard(part, o, h)
        sem = dcore.at[part] if kind == "core" else drecv.at[part, o, h]
        remote(ref, ref, dsend.at[part], sem, peer(kind)).start()

    def recv(part, o, h):
        ref = shard(part, o, h)
        remote(ref, ref, dsend.at[part], drecv.at[part, o, h], peer("core")).wait_recv()

    def core(part, o):
        send(part, o, None, "core")

    def first():
        for part in range(2):
            send(part, own, 0, "z")
            send(part, own, 1, "z")
            send(part, own, 0, "up")
            send(part, own, 1, "down")
            send(part, own, 1, "up")
            send(part, own, 0, "down")
        core(0, own)
        core(1, own)

    def pair(part):
        o = block(c, x, 1 - zl)
        recv(part, o, 0)
        send(part, o, 0, "up")
        send(part, o, 0, "down")
        recv(part, o, 1)
        send(part, o, 1, "down")
        send(part, o, 1, "up")

    def onward(part, zz):
        lo, hi = block(c, x3, zz), block(c, x1, zz)
        recv(part, lo, 0)
        send(part, lo, 0, "up")
        recv(part, hi, 1)
        send(part, hi, 1, "down")

    def near(part, zz):
        lo, hi = block(c, x3, zz), block(c, x1, zz)
        recv(part, lo, 1)
        core(part, lo)
        recv(part, hi, 0)
        core(part, hi)

    def far(part, zz):
        o = block(c, x2, zz)
        recv(part, o, 0)
        recv(part, o, 1)
        core(part, o)

    def other(part):
        ref = gu.at[pl.ds(8 * (1 - c), 8)] if part == 0 else dn.at[:, slots(8 * (1 - c), 8)]
        remote(ref, ref, dsend.at[part], dcore.at[part], peer("core")).wait_recv()

    first()

    loads[2].wait()
    loads[3].wait()
    lane = iota((256, 128), 1)
    name = iota((128, 64), 0)
    hit = jnp.concatenate(
        [
            ((routes_ref[s, 0:1, :] == name) | (routes_ref[s, 1:2, :] == name)).astype(F32).T
            for s in range(4)
        ],
        axis=0,
    )
    hitb = hit.astype(BF)
    ra, rb = iota((256, 256), 0), iota((256, 256), 1)
    before = ((rb < ra) & (ra // 64 == rb // 64)).astype(BF)
    pos = mm(before, hitb)
    expand = (iota((128, 256), 0) == iota((128, 256), 1) // CAP).astype(BF)
    hitx = mm(hitb, expand)
    posx = mm(pos.astype(BF), expand)
    ct = jnp.where(posx == (rb % CAP).astype(F32), hitx, 0.0)
    ctmat[...] = ct.astype(BF)
    cm = ct.T.astype(BF)
    cmat[...] = cm
    tok = tok_ref[...].reshape(256, 64)
    tok2 = jnp.concatenate([tok, tok], axis=1)
    want = iota((256, 128), 0) // 64
    half = lane // 64
    for j in range(2):
        placed = jnp.where(want == 2 * j + half, tok2.astype(F32), 0.0).astype(BF)
        msg[:, j] = mm(cm, placed).astype(BF).reshape(NE, CAP, 128)

    def zcopy(r, src):
        return remote(msg.at[pl.ds(2 * ((zh + r) % NZ), 2)], zm.at[src], zsend.at[r], zrecv.at[src], zdev(r))

    def zget(r):
        src = (zh + r) % NZ
        zcopy(r, src).wait_recv()
        yput(src)

    def yput(src):
        for r in FAR:
            to = (y + r) % NY
            remote(zm.at[src, to // 4], xr.at[src, y], ysend.at[src], yrecv.at[src], ydev(r)).start()
        pltpu.make_async_copy(zm.at[src, y // 4], xr.at[src, y], yrecv.at[src]).start()

    for r in (1, 3, 2):
        zcopy(r, zh).start()
    zm[zh] = msg[pl.ds(2 * zh, 2)]
    yput(zh)

    for cp in loads[4:7]:
        cp.wait()
    for cc in range(2):
        for xx in range(NX):
            for zz in range(2):
                s = (xx * 2 + cc) * 2 + zz
                b = block(cc, xx, zz)
                omrow[:, 128 * b : 128 * b + 128] = om_ref[:, 128 * s : 128 * s + 128]
    for u in range(16):
        grow[:, 128 * u : 128 * u + 128] = gain_ref[u : u + 1, :].astype(F32)

    def build(lo, hi):
        @pl.loop(lo, hi)
        def _(i):
            base = pl.multiple_of(i * 128, 128)
            perm[pl.ds(base, 128), :] = jnp.where(
                iota((128, D), 0) + base == omrow[...], 1.0, 0.0
            ).astype(BF)

    def build_back(lo, hi):
        @pl.loop(lo, hi)
        def _(i):
            here = jnp.broadcast_to(omrow[:, slots(i)].astype(F32), (128, 128)).T.astype(jnp.int32)
            rows = pl.ds(pl.multiple_of(F + i * 128, 128), 128)
            for u in range(16):
                ptw[rows, 128 * u : 128 * u + 128] = jnp.where(
                    iota((128, 128), 1) + 128 * u == here, 1.0, 0.0
                ).astype(BF)

    def turn():
        @pl.loop(0, 8)
        def _(i):
            at = pl.ds(pl.multiple_of(i * 256, 256), 256)
            ptw[:F, at] = w[at, 2 * F :].astype(F32).T.astype(BF)

    low = iota((64, 128), 1) < 64

    def quarter(r, carry):
        zz = (zh + r) % NZ
        remote(xr.at[zz], xr.at[zz], ysend.at[zz], yrecv.at[zz], ydev(1)).wait_recv()
        ssq, wacc, lacc = carry
        for u in range(NY // 2):
            a = xr[zz, 2 * u].reshape(64, 128).astype(F32)
            b = xr[zz, 2 * u + 1].reshape(64, 128).astype(F32)
            g = grow[:, pl.ds(pl.multiple_of(zz * ZB + 128 * u, 128), 128)]
            even = jnp.where(low, a, pltpu.roll(b, 64, 1))
            odd = jnp.where(low, pltpu.roll(a, 64, 1), b)
            ssq = ssq + jnp.concatenate([even * even, odd * odd], axis=0)
            xg[:64, 128 * u : 128 * u + 128] = (even * g).astype(BF)
            xg[64:, 128 * u : 128 * u + 128] = (odd * g).astype(BF)
        at = pl.ds(pl.multiple_of(zz * ZB, ZB), ZB)
        wacc = wacc + mm(xg[...], w[at, : 2 * F])
        lacc = lacc + mm(xg[...], router_ref[:, at], 1, 1)

        got = mm(xg[...], perm[at, :])
        if r == 0:
            xacc[...] = got
        elif r == 2:
            xp[...] = (xacc[...] + got).astype(BF)
        else:
            xacc[...] += got
        return ssq, wacc, lacc

    build(0, 8)
    pair(0)
    onward(0, zl)
    core(0, block(c, x, 1 - zl))
    zget(1)
    zget(3)
    pair(1)
    onward(1, zl)
    near(0, zl)
    core(1, block(c, x, 1 - zl))
    far(0, zl)
    zget(2)
    build(8, 16)
    onward(0, 1 - zl)
    loads[7].wait()
    turn()
    carry = (jnp.zeros((128, 128), F32), jnp.zeros((128, 2 * F), F32), jnp.zeros((128, NE), F32))
    carry = quarter(0, carry)
    onward(1, 1 - zl)
    near(1, zl)
    near(0, 1 - zl)
    build_back(0, 8)
    far(1, zl)
    carry = quarter(1, carry)
    far(0, 1 - zl)
    carry = quarter(3, carry)
    near(1, 1 - zl)
    build_back(8, 16)
    far(1, 1 - zl)
    ssq, wacc, lacc = quarter(2, carry)

    scale = lax.rsqrt(jnp.sum(ssq, axis=-1, keepdims=True) * (1.0 / D) + 1e-06)
    mine = cmat[pl.ds(pl.multiple_of(e0 * CAP, CAP), CAP), :].astype(F32)
    four = jnp.concatenate([mine, mine, mine, mine], axis=0)
    rowid = iota((128, 256), 0)
    step = (rowid // 32 % 2) * 2 + rowid // 64
    chosen = mm(jnp.where(iota((128, 256), 1) // 64 == step, four, 0.0).astype(BF), hitb)[:, :NE]
    sig = jax.nn.sigmoid(lacc * scale) * chosen
    total = jnp.sum(sig, axis=-1, keepdims=True)
    this = jnp.sum(jnp.where(iota((128, NE), 1) == e0, sig, 0.0), axis=-1, keepdims=True)
    used = jnp.sum(chosen, axis=-1, keepdims=True) > 0.5
    share = jnp.where(used, this / jnp.where(used, total, 1.0), 0.0)

    def halfmm(cc):
        at = pl.ds(pl.multiple_of(cc * (D // 2), D // 2), D // 2)
        return mm(xp[:, at], gu[pl.ds(8 * cc, 8)].reshape(D // 2, 2 * F))

    both = wacc + halfmm(c)
    other(0)
    both = (both + halfmm(1 - c)) * scale
    hidden = (jax.nn.silu(both[:, :F]) * both[:, F:] * share).astype(BF)
    hy[:, :F] = hidden
    other(1)
    hy[:, F:] = mm(hidden, dn[...]).astype(BF)

    for r in (1, 2, 3, 0):
        zz = (zh + r) % NZ
        at = pl.ds(pl.multiple_of(zz * ZB, ZB), ZB)
        part = mm(hy[...], ptw[:, at])
        for u in range(NY // 2):
            even, odd = part[:64, 128 * u : 128 * u + 128], part[64:, 128 * u : 128 * u + 128]
            outm[zz, 2 * u] = jnp.where(low, even, pltpu.roll(odd, 64, 1)).astype(BF).reshape(2, CAP, 128)
            outm[zz, 2 * u + 1] = jnp.where(low, pltpu.roll(even, 64, 1), odd).astype(BF).reshape(2, CAP, 128)
        for k in FAR:
            remote(outm.at[zz, (y + k) % NY], outr.at[zz, y], osend.at[r], orecv.at[zz], ydev(k)).start()
        pltpu.make_async_copy(outm.at[zz, y], outr.at[zz, y], orecv.at[zz]).start()

    def sums(r):
        zz = (zh + r) % NZ
        remote(outr.at[zz], outr.at[zz], osend.at[r], orecv.at[zz], ydev(1)).wait_recv()
        got = outr[zz].astype(F32)
        return jnp.stack([jnp.sum(got[:4], axis=0), jnp.sum(got[4:], axis=0)]).astype(BF)

    def pcopy(r, src):
        return remote(zs.at[r], zr.at[src], psend.at[r], precv.at[src], zdev(r))

    for r in (1, 2, 3):
        zs[r] = sums(r)
        pcopy(r, zh).start()
    zr[zh] = sums(0)
    for r in (1, 2, 3):
        pcopy(r, (zh + r) % NZ).wait_recv()

    for j in range(2):
        acc = mm(ctmat[128 * j : 128 * j + 128, :], zr[:, :, j].reshape(256, 128))
        for a in range(2):
            s = 2 * j + a
            out_ref[s] = (
                tok_ref[s].astype(F32) + acc[64 * a : 64 * a + 64, 64 * a : 64 * a + 64]
            ).astype(BF)

    for r in (1, 2, 3):
        zcopy(r, zh).wait_send()
        pcopy(r, zh).wait_send()
    for part in range(2):
        ref = gu.at[pl.ds(0, 15)] if part == 0 else dn.at[:, pl.ds(0, 15 * 128)]
        remote(ref, ref, dsend.at[part], dcore.at[part], peer("core")).wait_send()
    for r in range(NZ):
        ref = xr.at[r, pl.ds(0, NY - 1)]
        remote(ref, ref, ysend.at[r], yrecv.at[r], ydev(1)).wait_send()
        remote(ref, ref, osend.at[r], orecv.at[r], ydev(1)).wait_send()


def body(tokens, norm_gain, router, routes, expert_weights, codes, scales, owner_map):
    dma = pltpu.SemaphoreType.DMA
    vm = pltpu.VMEM
    return pl.pallas_call(
        kernel,
        out_shape=jax.ShapeDtypeStruct(tokens.shape, BF),
        in_specs=[pl.BlockSpec(memory_space=pltpu.HBM)] * 8,
        out_specs=pl.BlockSpec(memory_space=pltpu.VMEM),
        scratch_shapes=[
            vm((4, 64, 64), BF),
            vm((16, 128), BF),
            vm((NE, D), BF),
            vm((4, 2, 64), jnp.int32),
            vm((128, 3 * F), BF),
            vm((48, 128), BF),
            vm((1, D), jnp.int32),
            vm((1, D), F32),
            vm((1, D), jnp.int32),
            vm((D, 3 * F), BF),
            vm((16, 128, 2 * F), BF),
            vm((F, D), BF),
            vm((D, D), BF),
            vm((F + D, D), BF),
            vm((128, F + D), BF),
            vm((256, 256), BF),
            vm((256, 256), BF),
            vm((NE, 2, CAP, 128), BF),
            vm((NZ, 2, 2, CAP, 128), BF),
            vm((NZ, NY, 2, CAP, 128), BF),
            vm((128, ZB), BF),
            vm((128, D), F32),
            vm((128, D), BF),
            vm((NZ, NY, 2, CAP, 128), BF),
            vm((NZ, NY, 2, CAP, 128), BF),
            vm((NZ, 2, 2, CAP, 128), BF),
            vm((NZ, 2, 2, CAP, 128), BF),
            dma((8,)), dma((2,)), dma((2, 16, 2)), dma((2,)),
            dma((NZ,)), dma((NZ,)), dma((NZ,)), dma((NZ,)),
            dma((NZ,)), dma((NZ,)), dma((NZ,)), dma((NZ,)),
        ],
        compiler_params=pltpu.CompilerParams(
            collective_id=0, has_side_effects=True, vmem_limit_bytes=60 << 20
        ),
        cost_estimate=pl.CostEstimate(flops=4 * 10**9, bytes_accessed=8 << 20, transcendentals=0),
    )(
        tokens, norm_gain.reshape(16, 128), router.T, routes.transpose(0, 2, 1), expert_weights,
        codes, scales.transpose(0, 2, 1), owner_map.reshape(1, D),
    )


def solution(mesh):
    placed = (
        P(None, ("rep", "fsdp"), "tp"),
        P(),
        P(),
        P(None, ("rep", "fsdp"), None),
        P("tp", None, None),
        P("tp", ("rep", "fsdp"), None),
        P("tp", ("rep", "fsdp"), None),
        P(),
    )
    return jax.shard_map(
        body, mesh=mesh, in_specs=placed, out_specs=P(None, ("rep", "fsdp"), "tp"), check_vma=False
    )
```

```python
import jax
import jax.numpy as jnp
from jax import lax
from jax.experimental import pallas as pl
from jax.experimental.pallas import tpu as pltpu
from jax.sharding import PartitionSpec as P

MESH = pl.DeviceIdType.MESH
BF = jnp.bfloat16
F32 = jnp.float32
NX, NZ, NY, NE, CAP = 4, 4, 8, 8, 32
D, F = 2048, 256
ZB = D // NZ
FAR = (4, 3, 5, 2, 6, 1, 7)


def mm(a, b, ca=1, cb=0):
    return lax.dot_general(a, b, (((ca,), (cb,)), ((), ())), preferred_element_type=F32)


def iota(shape, dim):
    return lax.broadcasted_iota(jnp.int32, shape, dim)


def kernel(
    tok_hbm, gain_hbm, router_hbm, routes_hbm, w_hbm, codes_hbm, scales_hbm, om_hbm, out_ref,
    tok_ref, gain_ref, router_ref, routes_ref, codes_ref, scales_ref, om_ref, grow, omrow,
    w, gu, dn, perm, ptw, hy, cmat, ctmat, msg, zm, xr, xg, xacc, xp, outm, outr, zs, zr,
    wsem, dsend, drecv, dcore, zsend, zrecv, ysend, yrecv, osend, orecv, psend, precv,
):
    rep, tp, zl = lax.axis_index("rep"), lax.axis_index("tp"), lax.axis_index("fsdp")
    x, c = rep // 2, rep % 2
    zh, y = tp // NY, tp % NY
    e0 = tp // 4
    x1, x2, x3 = (x + 1) % NX, (x + 2) % NX, (x + 3) % NX

    def peer(kind):
        if kind == "core":
            return {"rep": x * 2 + (1 - c)}
        if kind == "z":
            return {"fsdp": 1 - zl}
        return {"rep": (x1 if kind == "up" else x3) * 2 + c}

    def ydev(r):
        return {"tp": zh * NY + (y + r) % NY}

    def zdev(r):
        return {"tp": ((zh + r) % NZ) * NY + y}

    def remote(src, dst, ssem, rsem, dev):
        return pltpu.make_async_remote_copy(
            src_ref=src, dst_ref=dst, send_sem=ssem, recv_sem=rsem, device_id=dev,
            device_id_type=MESH,
        )

    pairs = (
        (scales_hbm.at[0], scales_ref), (codes_hbm.at[0], codes_ref), (routes_hbm, routes_ref),
        (tok_hbm, tok_ref), (om_hbm, om_ref), (router_hbm, router_ref), (gain_hbm, gain_ref),
        (w_hbm.at[0], w),
    )
    loads = [pltpu.make_async_copy(a, b, wsem.at[i]) for i, (a, b) in enumerate(pairs)]
    loads[0].start()
    loads[1].start()

    bar = pltpu.get_barrier_semaphore()
    partners = [peer(k) for k in ("core", "z", "up", "down")]
    partners += [ydev(r) for r in range(1, NY)] + [zdev(r) for r in range(1, NZ)]
    for dev in partners:
        pl.semaphore_signal(bar, inc=1, device_id=dev, device_id_type=MESH)
    for cp in loads[2:]:
        cp.start()

    loads[0].wait()
    loads[1].wait()

    def block(cc, xx, zz):
        return cc * 8 + xx * 2 + zz

    def slots(b, n=1):
        return pl.ds(pl.multiple_of(b * 128, 128), n * 128)

    own = block(c, x, zl)
    spread = (iota((48, 768), 1) // 16 == iota((48, 768), 0)).astype(BF)
    delta = codes_ref[...].astype(F32) * mm(scales_ref[...], spread, 0, 0)
    gu[own] = delta[:, : 2 * F].astype(BF)
    dn[:, slots(own)] = delta[:, 2 * F :].T.astype(BF)

    pl.semaphore_wait(bar, len(partners))

    def shard(part, o, h):
        if part == 0:
            return gu.at[o] if h is None else gu.at[o, pl.ds(64 * h, 64)]
        return dn.at[:, slots(o)] if h is None else dn.at[pl.ds(128 * h, 128), slots(o)]

    def send(part, o, h, kind):
        ref = shard(part, o, h)
        sem = dcore.at[part] if kind == "core" else drecv.at[part, o, h]
        remote(ref, ref, dsend.at[part], sem, peer(kind)).start()

    def recv(part, o, h):
        ref = shard(part, o, h)
        remote(ref, ref, dsend.at[part], drecv.at[part, o, h], peer("core")).wait_recv()

    def core(part, o):
        send(part, o, None, "core")

    def over(o):
        remote(shard(1, o, None), shard(1, o, None), dsend.at[1], drecv.at[1, o, 0], peer("z")).start()

    def both_ways(part):
        send(part, own, 0, "up")
        send(part, own, 1, "down")
        send(part, own, 1, "up")
        send(part, own, 0, "down")

    def first():
        send(0, own, 0, "z")
        send(0, own, 1, "z")
        both_ways(1)
        both_ways(0)
        over(own)
        core(1, own)
        core(0, own)

    def pair(part):
        o = block(c, x, 1 - zl)
        recv(part, o, 0)
        send(part, o, 0, "up")
        send(part, o, 0, "down")
        recv(part, o, 1)
        send(part, o, 1, "down")
        send(part, o, 1, "up")

    def onward(part, zz):
        lo, hi = block(c, x3, zz), block(c, x1, zz)
        recv(part, lo, 0)
        send(part, lo, 0, "up")
        recv(part, hi, 1)
        send(part, hi, 1, "down")

    def near(part, zz):
        lo, hi = block(c, x3, zz), block(c, x1, zz)
        recv(part, lo, 1)
        if part == 1:
            over(lo)
        else:
            core(part, lo)
        recv(part, hi, 0)
        if part == 1:
            over(hi)
        else:
            core(part, hi)

    def far(part, zz):
        o = block(c, x2, zz)
        recv(part, o, 0)
        recv(part, o, 1)
        if part == 1:
            over(o)
        core(part, o)

    def across():
        for xx in (x, x3, x1, x2):
            o = block(c, xx, 1 - zl)
            ref = shard(1, o, None)
            remote(ref, ref, dsend.at[1], drecv.at[1, o, 0], peer("core")).wait_recv()
            core(1, o)

    def other(part):
        ref = gu.at[pl.ds(8 * (1 - c), 8)] if part == 0 else dn.at[:, slots(8 * (1 - c), 8)]
        remote(ref, ref, dsend.at[part], dcore.at[part], peer("core")).wait_recv()

    first()

    loads[2].wait()
    loads[3].wait()
    lane = iota((256, 128), 1)
    name = iota((128, 64), 0)
    hit = jnp.concatenate(
        [
            ((routes_ref[s, 0:1, :] == name) | (routes_ref[s, 1:2, :] == name)).astype(F32).T
            for s in range(4)
        ],
        axis=0,
    )
    hitb = hit.astype(BF)
    ra, rb = iota((256, 256), 0), iota((256, 256), 1)
    before = ((rb < ra) & (ra // 64 == rb // 64)).astype(BF)
    pos = mm(before, hitb)
    expand = (iota((128, 256), 0) == iota((128, 256), 1) // CAP).astype(BF)
    hitx = mm(hitb, expand)
    posx = mm(pos.astype(BF), expand)
    ct = jnp.where(posx == (rb % CAP).astype(F32), hitx, 0.0)
    ctmat[...] = ct.astype(BF)
    cm = ct.T.astype(BF)
    cmat[...] = cm
    tok = tok_ref[...].reshape(256, 64)
    tok2 = jnp.concatenate([tok, tok], axis=1)
    want = iota((256, 128), 0) // 64
    half = lane // 64
    for j in range(2):
        placed = jnp.where(want == 2 * j + half, tok2.astype(F32), 0.0).astype(BF)
        msg[:, j] = mm(cm, placed).astype(BF).reshape(NE, CAP, 128)

    def zcopy(r, src):
        return remote(msg.at[pl.ds(2 * ((zh + r) % NZ), 2)], zm.at[src], zsend.at[r], zrecv.at[src], zdev(r))

    def zget(r):
        src = (zh + r) % NZ
        zcopy(r, src).wait_recv()
        yput(src)

    def yput(src):
        for r in FAR:
            to = (y + r) % NY
            remote(zm.at[src, to // 4], xr.at[src, y], ysend.at[src], yrecv.at[src], ydev(r)).start()
        pltpu.make_async_copy(zm.at[src, y // 4], xr.at[src, y], yrecv.at[src]).start()

    for r in (1, 3, 2):
        zcopy(r, zh).start()
    zm[zh] = msg[pl.ds(2 * zh, 2)]
    yput(zh)

    for cp in loads[4:7]:
        cp.wait()
    for cc in range(2):
        for xx in range(NX):
            for zz in range(2):
                s = (xx * 2 + cc) * 2 + zz
                b = block(cc, xx, zz)
                omrow[:, 128 * b : 128 * b + 128] = om_ref[:, 128 * s : 128 * s + 128]
    for u in range(16):
        grow[:, 128 * u : 128 * u + 128] = gain_ref[u : u + 1, :].astype(F32)

    def build(lo, hi):
        @pl.loop(lo, hi)
        def _(i):
            base = pl.multiple_of(i * 128, 128)
            perm[pl.ds(base, 128), :] = jnp.where(
                iota((128, D), 0) + base == omrow[...], 1.0, 0.0
            ).astype(BF)

    def build_back(lo, hi):
        @pl.loop(lo, hi)
        def _(i):
            here = jnp.broadcast_to(omrow[:, slots(i)].astype(F32), (128, 128)).T.astype(jnp.int32)
            rows = pl.ds(pl.multiple_of(F + i * 128, 128), 128)
            for u in range(16):
                ptw[rows, 128 * u : 128 * u + 128] = jnp.where(
                    iota((128, 128), 1) + 128 * u == here, 1.0, 0.0
                ).astype(BF)

    def turn():
        @pl.loop(0, 8)
        def _(i):
            at = pl.ds(pl.multiple_of(i * 256, 256), 256)
            ptw[:F, at] = w[at, 2 * F :].astype(F32).T.astype(BF)

    low = iota((64, 128), 1) < 64

    def quarter(r, carry):
        zz = (zh + r) % NZ
        remote(xr.at[zz], xr.at[zz], ysend.at[zz], yrecv.at[zz], ydev(1)).wait_recv()
        ssq, wacc, lacc = carry
        for u in range(NY // 2):
            a = xr[zz, 2 * u].reshape(64, 128).astype(F32)
            b = xr[zz, 2 * u + 1].reshape(64, 128).astype(F32)
            g = grow[:, pl.ds(pl.multiple_of(zz * ZB + 128 * u, 128), 128)]
            even = jnp.where(low, a, pltpu.roll(b, 64, 1))
            odd = jnp.where(low, pltpu.roll(a, 64, 1), b)
            ssq = ssq + jnp.concatenate([even * even, odd * odd], axis=0)
            xg[:64, 128 * u : 128 * u + 128] = (even * g).astype(BF)
            xg[64:, 128 * u : 128 * u + 128] = (odd * g).astype(BF)
        at = pl.ds(pl.multiple_of(zz * ZB, ZB), ZB)
        wacc = wacc + mm(xg[...], w[at, : 2 * F])
        lacc = lacc + mm(xg[...], router_ref[:, at], 1, 1)

        got = mm(xg[...], perm[at, :])
        if r == 0:
            xacc[...] = got
        elif r == 2:
            xp[...] = (xacc[...] + got).astype(BF)
        else:
            xacc[...] += got
        return ssq, wacc, lacc

    build(0, 16)
    loads[7].wait()
    turn()
    mine = cmat[pl.ds(pl.multiple_of(e0 * CAP, CAP), CAP), :].astype(F32)
    four = jnp.concatenate([mine, mine, mine, mine], axis=0)
    rowid = iota((128, 256), 0)
    step = (rowid // 32 % 2) * 2 + rowid // 64
    chosen = mm(jnp.where(iota((128, 256), 1) // 64 == step, four, 0.0).astype(BF), hitb)[:, :NE]
    build_back(0, 8)

    onward(1, zl)
    pair(0)
    near(1, zl)
    onward(0, zl)
    build_back(8, 16)
    core(1, block(c, x3, zl))
    core(1, block(c, x1, zl))
    core(0, block(c, x, 1 - zl))
    zget(1)
    zget(3)
    far(1, zl)
    near(0, zl)
    zget(2)
    onward(0, 1 - zl)
    far(0, zl)
    carry = (jnp.zeros((128, 128), F32), jnp.zeros((128, 2 * F), F32), jnp.zeros((128, NE), F32))
    carry = quarter(0, carry)
    across()
    near(0, 1 - zl)
    carry = quarter(1, carry)
    far(0, 1 - zl)
    carry = quarter(3, carry)
    ssq, wacc, lacc = quarter(2, carry)

    scale = lax.rsqrt(jnp.sum(ssq, axis=-1, keepdims=True) * (1.0 / D) + 1e-06)
    sig = jax.nn.sigmoid(lacc * scale) * chosen
    total = jnp.sum(sig, axis=-1, keepdims=True)
    this = jnp.sum(jnp.where(iota((128, NE), 1) == e0, sig, 0.0), axis=-1, keepdims=True)
    used = jnp.sum(chosen, axis=-1, keepdims=True) > 0.5
    share = jnp.where(used, this / jnp.where(used, total, 1.0), 0.0)

    def halfmm(cc):
        at = pl.ds(pl.multiple_of(cc * (D // 2), D // 2), D // 2)
        return mm(xp[:, at], gu[pl.ds(8 * cc, 8)].reshape(D // 2, 2 * F))

    both = wacc + halfmm(c)
    other(0)
    both = (both + halfmm(1 - c)) * scale
    hidden = (jax.nn.silu(both[:, :F]) * both[:, F:] * share).astype(BF)
    hy[:, :F] = hidden
    other(1)
    hy[:, F:] = mm(hidden, dn[...]).astype(BF)

    for r in (1, 2, 3, 0):
        zz = (zh + r) % NZ
        at = pl.ds(pl.multiple_of(zz * ZB, ZB), ZB)
        part = mm(hy[...], ptw[:, at])
        for u in range(NY // 2):
            even, odd = part[:64, 128 * u : 128 * u + 128], part[64:, 128 * u : 128 * u + 128]
            outm[zz, 2 * u] = jnp.where(low, even, pltpu.roll(odd, 64, 1)).astype(BF).reshape(2, CAP, 128)
            outm[zz, 2 * u + 1] = jnp.where(low, pltpu.roll(even, 64, 1), odd).astype(BF).reshape(2, CAP, 128)
        for k in FAR:
            remote(outm.at[zz, (y + k) % NY], outr.at[zz, y], osend.at[r], orecv.at[zz], ydev(k)).start()
        pltpu.make_async_copy(outm.at[zz, y], outr.at[zz, y], orecv.at[zz]).start()

    def sums(r):
        zz = (zh + r) % NZ
        remote(outr.at[zz], outr.at[zz], osend.at[r], orecv.at[zz], ydev(1)).wait_recv()
        got = outr[zz].astype(F32)
        return jnp.stack([jnp.sum(got[:4], axis=0), jnp.sum(got[4:], axis=0)]).astype(BF)

    def pcopy(r, src):
        return remote(zs.at[r], zr.at[src], psend.at[r], precv.at[src], zdev(r))

    for r in (1, 2, 3):
        zs[r] = sums(r)
        pcopy(r, zh).start()
    zr[zh] = sums(0)
    for r in (1, 2, 3):
        pcopy(r, (zh + r) % NZ).wait_recv()

    for j in range(2):
        acc = mm(ctmat[128 * j : 128 * j + 128, :], zr[:, :, j].reshape(256, 128))
        for a in range(2):
            s = 2 * j + a
            out_ref[s] = (
                tok_ref[s].astype(F32) + acc[64 * a : 64 * a + 64, 64 * a : 64 * a + 64]
            ).astype(BF)

    for r in (1, 2, 3):
        zcopy(r, zh).wait_send()
        pcopy(r, zh).wait_send()
    for part in range(2):
        ref = gu.at[pl.ds(0, 15)] if part == 0 else dn.at[:, pl.ds(0, 15 * 128)]
        remote(ref, ref, dsend.at[part], dcore.at[part], peer("core")).wait_send()
    for r in range(NZ):
        ref = xr.at[r, pl.ds(0, NY - 1)]
        remote(ref, ref, ysend.at[r], yrecv.at[r], ydev(1)).wait_send()
        remote(ref, ref, osend.at[r], orecv.at[r], ydev(1)).wait_send()


def body(tokens, norm_gain, router, routes, expert_weights, codes, scales, owner_map):
    dma = pltpu.SemaphoreType.DMA
    vm = pltpu.VMEM
    return pl.pallas_call(
        kernel,
        out_shape=jax.ShapeDtypeStruct(tokens.shape, BF),
        in_specs=[pl.BlockSpec(memory_space=pltpu.HBM)] * 8,
        out_specs=pl.BlockSpec(memory_space=pltpu.VMEM),
        scratch_shapes=[
            vm((4, 64, 64), BF),
            vm((16, 128), BF),
            vm((NE, D), BF),
            vm((4, 2, 64), jnp.int32),
            vm((128, 3 * F), BF),
            vm((48, 128), BF),
            vm((1, D), jnp.int32),
            vm((1, D), F32),
            vm((1, D), jnp.int32),
            vm((D, 3 * F), BF),
            vm((16, 128, 2 * F), BF),
            vm((F, D), BF),
            vm((D, D), BF),
            vm((F + D, D), BF),
            vm((128, F + D), BF),
            vm((256, 256), BF),
            vm((256, 256), BF),
            vm((NE, 2, CAP, 128), BF),
            vm((NZ, 2, 2, CAP, 128), BF),
            vm((NZ, NY, 2, CAP, 128), BF),
            vm((128, ZB), BF),
            vm((128, D), F32),
            vm((128, D), BF),
            vm((NZ, NY, 2, CAP, 128), BF),
            vm((NZ, NY, 2, CAP, 128), BF),
            vm((NZ, 2, 2, CAP, 128), BF),
            vm((NZ, 2, 2, CAP, 128), BF),
            dma((8,)), dma((2,)), dma((2, 16, 2)), dma((2,)),
            dma((NZ,)), dma((NZ,)), dma((NZ,)), dma((NZ,)),
            dma((NZ,)), dma((NZ,)), dma((NZ,)), dma((NZ,)),
        ],
        compiler_params=pltpu.CompilerParams(
            collective_id=0, has_side_effects=True, vmem_limit_bytes=60 << 20
        ),
        cost_estimate=pl.CostEstimate(flops=4 * 10**9, bytes_accessed=8 << 20, transcendentals=0),
    )(
        tokens, norm_gain.reshape(16, 128), router.T, routes.transpose(0, 2, 1), expert_weights,
        codes, scales.transpose(0, 2, 1), owner_map.reshape(1, D),
    )


def solution(mesh):
    placed = (
        P(None, ("rep", "fsdp"), "tp"),
        P(),
        P(),
        P(None, ("rep", "fsdp"), None),
        P("tp", None, None),
        P("tp", ("rep", "fsdp"), None),
        P("tp", ("rep", "fsdp"), None),
        P(),
    )
    return jax.shard_map(
        body, mesh=mesh, in_specs=placed, out_specs=P(None, ("rep", "fsdp"), "tp"), check_vma=False
    )
```

```python
import jax
import jax.numpy as jnp
from jax import lax
from jax.experimental import pallas as pl
from jax.experimental.pallas import tpu as pltpu
from jax.sharding import PartitionSpec as P

MESH = pl.DeviceIdType.MESH
BF = jnp.bfloat16
F32 = jnp.float32
NX, NZ, NY, NE, CAP = 4, 4, 8, 8, 32
D, F = 2048, 256
ZB = D // NZ
FAR = (4, 3, 5, 2, 6, 1, 7)


def mm(a, b, ca=1, cb=0):
    return lax.dot_general(a, b, (((ca,), (cb,)), ((), ())), preferred_element_type=F32)


def iota(shape, dim):
    return lax.broadcasted_iota(jnp.int32, shape, dim)


def kernel(
    tok_hbm, gain_hbm, router_hbm, routes_hbm, w_hbm, codes_hbm, scales_hbm, om_hbm, out_ref,
    tok_ref, gain_ref, router_ref, routes_ref, codes_ref, scales_ref, om_ref, grow, omrow,
    wd, gu, dn, wide, ptw, hy, cmat, ctmat, msg, zm, xr, xg, xacc, xp, outm, outr, zs, zr,
    wsem, dsend, drecv, dcore, zsend, zrecv, ysend, yrecv, osend, orecv, psend, precv,
):
    rep, tp, zl = lax.axis_index("rep"), lax.axis_index("tp"), lax.axis_index("fsdp")
    x, c = rep // 2, rep % 2
    zh, y = tp // NY, tp % NY
    e0 = tp // 4
    x1, x2, x3 = (x + 1) % NX, (x + 2) % NX, (x + 3) % NX

    def peer(kind):
        if kind == "core":
            return {"rep": x * 2 + (1 - c)}
        if kind == "z":
            return {"fsdp": 1 - zl}
        return {"rep": (x1 if kind == "up" else x3) * 2 + c}

    def ydev(r):
        return {"tp": zh * NY + (y + r) % NY}

    def zdev(r):
        return {"tp": ((zh + r) % NZ) * NY + y}

    def remote(src, dst, ssem, rsem, dev):
        return pltpu.make_async_remote_copy(
            src_ref=src, dst_ref=dst, send_sem=ssem, recv_sem=rsem, device_id=dev,
            device_id_type=MESH,
        )

    pairs = (
        (scales_hbm.at[0], scales_ref), (codes_hbm.at[0], codes_ref), (routes_hbm, routes_ref),
        (tok_hbm, tok_ref), (om_hbm, om_ref), (router_hbm, router_ref), (gain_hbm, gain_ref),
        (w_hbm.at[0, :, pl.ds(0, 2 * F)], wide.at[:, pl.ds(D, 2 * F)]),
        (w_hbm.at[0, :, pl.ds(2 * F, F)], wd),
    )
    loads = [pltpu.make_async_copy(a, b, wsem.at[i]) for i, (a, b) in enumerate(pairs)]
    loads[0].start()
    loads[1].start()

    bar = pltpu.get_barrier_semaphore()
    partners = [ydev(4), zdev(2), ydev(3), ydev(5), zdev(1), zdev(3)]
    partners += [peer(k) for k in ("z", "up", "down", "core")] + [ydev(r) for r in (2, 6, 1, 7)]
    for dev in partners:
        pl.semaphore_signal(bar, inc=1, device_id=dev, device_id_type=MESH)
    for cp in loads[2:]:
        cp.start()

    loads[0].wait()
    loads[1].wait()

    def block(cc, xx, zz):
        return cc * 8 + xx * 2 + zz

    def slots(b, n=1):
        return pl.ds(pl.multiple_of(b * 128, 128), n * 128)

    own = block(c, x, zl)
    spread = (iota((48, 768), 1) // 16 == iota((48, 768), 0)).astype(BF)
    delta = codes_ref[...].astype(F32) * mm(scales_ref[...], spread, 0, 0)
    gu[own] = delta[:, : 2 * F].astype(BF)
    dn[:, slots(own)] = delta[:, 2 * F :].T.astype(BF)

    pl.semaphore_wait(bar, len(partners))

    def shard(part, o, h):
        if part == 0:
            return gu.at[o] if h is None else gu.at[o, pl.ds(64 * h, 64)]
        return dn.at[:, slots(o)] if h is None else dn.at[pl.ds(128 * h, 128), slots(o)]

    def send(part, o, h, kind):
        ref = shard(part, o, h)
        sem = dcore.at[part] if kind == "core" else drecv.at[part, o, h]
        remote(ref, ref, dsend.at[part], sem, peer(kind)).start()

    def recv(part, o, h):
        ref = shard(part, o, h)
        remote(ref, ref, dsend.at[part], drecv.at[part, o, h], peer("core")).wait_recv()

    def core(part, o):
        send(part, o, None, "core")

    def over(o):
        remote(shard(1, o, None), shard(1, o, None), dsend.at[1], drecv.at[1, o, 0], peer("z")).start()

    def both_ways(part):
        send(part, own, 0, "up")
        send(part, own, 1, "down")
        send(part, own, 1, "up")
        send(part, own, 0, "down")

    def first():
        send(0, own, 0, "z")
        send(0, own, 1, "z")
        both_ways(1)
        both_ways(0)
        over(own)
        core(1, own)
        core(0, own)

    def pair(part):
        o = block(c, x, 1 - zl)
        recv(part, o, 0)
        send(part, o, 0, "up")
        send(part, o, 0, "down")
        recv(part, o, 1)
        send(part, o, 1, "down")
        send(part, o, 1, "up")

    def onward(part, zz):
        lo, hi = block(c, x3, zz), block(c, x1, zz)
        recv(part, lo, 0)
        send(part, lo, 0, "up")
        recv(part, hi, 1)
        send(part, hi, 1, "down")

    def near(part, zz):
        lo, hi = block(c, x3, zz), block(c, x1, zz)
        recv(part, lo, 1)
        if part == 1:
            over(lo)
        else:
            core(part, lo)
        recv(part, hi, 0)
        if part == 1:
            over(hi)
        else:
            core(part, hi)

    def far(part, zz):
        o = block(c, x2, zz)
        recv(part, o, 0)
        recv(part, o, 1)
        if part == 1:
            over(o)
        core(part, o)

    def across():
        for xx in (x, x3, x1, x2):
            o = block(c, xx, 1 - zl)
            ref = shard(1, o, None)
            remote(ref, ref, dsend.at[1], drecv.at[1, o, 0], peer("core")).wait_recv()
            core(1, o)

    def other(part):
        ref = gu.at[pl.ds(8 * (1 - c), 8)] if part == 0 else dn.at[:, slots(8 * (1 - c), 8)]
        remote(ref, ref, dsend.at[part], dcore.at[part], peer("core")).wait_recv()

    first()

    loads[2].wait()
    loads[3].wait()
    lane = iota((256, 128), 1)
    name = iota((128, 64), 0)
    hit = jnp.concatenate(
        [
            ((routes_ref[s, 0:1, :] == name) | (routes_ref[s, 1:2, :] == name)).astype(F32).T
            for s in range(4)
        ],
        axis=0,
    )
    hitb = hit.astype(BF)
    ra, rb = iota((256, 256), 0), iota((256, 256), 1)
    before = ((rb < ra) & (ra // 64 == rb // 64)).astype(BF)
    pos = mm(before, hitb)
    expand = (iota((128, 256), 0) == iota((128, 256), 1) // CAP).astype(BF)
    hitx = mm(hitb, expand)
    posx = mm(pos.astype(BF), expand)
    ct = jnp.where(posx == (rb % CAP).astype(F32), hitx, 0.0)
    ctmat[...] = ct.astype(BF)
    cm = ct.T.astype(BF)
    cmat[...] = cm
    tok = tok_ref[...].reshape(256, 64)
    tok2 = jnp.concatenate([tok, tok], axis=1)
    want = iota((256, 128), 0) // 64
    half = lane // 64
    for j in range(2):
        placed = jnp.where(want == 2 * j + half, tok2.astype(F32), 0.0).astype(BF)
        msg[:, j] = mm(cm, placed).astype(BF).reshape(NE, CAP, 128)

    def zcopy(r, src):
        return remote(msg.at[pl.ds(2 * ((zh + r) % NZ), 2)], zm.at[src], zsend.at[r], zrecv.at[src], zdev(r))

    def zget(r):
        src = (zh + r) % NZ
        zcopy(r, src).wait_recv()
        yput(src)

    def yput(src):
        for r in FAR:
            to = (y + r) % NY
            remote(zm.at[src, to // 4], xr.at[src, y], ysend.at[src], yrecv.at[src], ydev(r)).start()
        pltpu.make_async_copy(zm.at[src, y // 4], xr.at[src, y], yrecv.at[src]).start()

    for r in (1, 3, 2):
        zcopy(r, zh).start()
    zm[zh] = msg[pl.ds(2 * zh, 2)]
    yput(zh)

    for cp in loads[4:7]:
        cp.wait()
    for cc in range(2):
        for xx in range(NX):
            for zz in range(2):
                s = (xx * 2 + cc) * 2 + zz
                b = block(cc, xx, zz)
                omrow[:, 128 * b : 128 * b + 128] = om_ref[:, 128 * s : 128 * s + 128]
    for u in range(16):
        grow[:, 128 * u : 128 * u + 128] = gain_ref[u : u + 1, :].astype(F32)

    def build(lo, hi):
        @pl.loop(lo, hi)
        def _(i):
            base = pl.multiple_of(i * 128, 128)
            wide[pl.ds(base, 128), :D] = jnp.where(
                iota((128, D), 0) + base == omrow[...], 1.0, 0.0
            ).astype(BF)

    def build_back(lo, hi):
        @pl.loop(lo, hi)
        def _(i):
            here = jnp.broadcast_to(omrow[:, slots(i)].astype(F32), (128, 128)).T.astype(jnp.int32)
            rows = pl.ds(pl.multiple_of(F + i * 128, 128), 128)
            for u in range(16):
                ptw[rows, 128 * u : 128 * u + 128] = jnp.where(
                    iota((128, 128), 1) + 128 * u == here, 1.0, 0.0
                ).astype(BF)

    def turn():
        @pl.loop(0, 8)
        def _(i):
            at = pl.ds(pl.multiple_of(i * 256, 256), 256)
            ptw[:F, at] = wd[at, :].astype(F32).T.astype(BF)

    low = iota((64, 128), 1) < 64

    def quarter(r, ssq):
        zz = (zh + r) % NZ
        remote(xr.at[zz], xr.at[zz], ysend.at[zz], yrecv.at[zz], ydev(1)).wait_recv()
        for u in range(NY // 2):
            a = xr[zz, 2 * u].reshape(64, 128).astype(F32)
            b = xr[zz, 2 * u + 1].reshape(64, 128).astype(F32)
            g = grow[:, pl.ds(pl.multiple_of(zz * ZB + 128 * u, 128), 128)]
            even = jnp.where(low, a, pltpu.roll(b, 64, 1))
            odd = jnp.where(low, pltpu.roll(a, 64, 1), b)
            ssq = ssq + jnp.concatenate([even * even, odd * odd], axis=0)
            xg[:64, 128 * u : 128 * u + 128] = (even * g).astype(BF)
            xg[64:, 128 * u : 128 * u + 128] = (odd * g).astype(BF)
        at = pl.ds(pl.multiple_of(zz * ZB, ZB), ZB)
        got = mm(xg[...], wide[at, :])
        if r == 0:
            xacc[...] = got
        else:
            xacc[...] += got
        return ssq

    build(0, 16)
    loads[7].wait()
    loads[8].wait()
    turn()
    for u in range(16):
        names = router_ref[:, 128 * u : 128 * u + 128].astype(F32)
        tall = jnp.concatenate([names, jnp.zeros((128 - NE, 128), F32)], axis=0)
        wide[128 * u : 128 * u + 128, D + 2 * F :] = tall.T.astype(BF)
    mine = cmat[pl.ds(pl.multiple_of(e0 * CAP, CAP), CAP), :].astype(F32)
    four = jnp.concatenate([mine, mine, mine, mine], axis=0)
    rowid = iota((128, 256), 0)
    step = (rowid // 32 % 2) * 2 + rowid // 64
    chosen = mm(jnp.where(iota((128, 256), 1) // 64 == step, four, 0.0).astype(BF), hitb)[:, :NE]
    build_back(0, 8)

    onward(1, zl)
    pair(0)
    near(1, zl)
    onward(0, zl)
    build_back(8, 16)
    core(1, block(c, x3, zl))
    core(1, block(c, x1, zl))
    core(0, block(c, x, 1 - zl))
    zget(1)
    zget(3)
    far(1, zl)
    near(0, zl)
    zget(2)
    onward(0, 1 - zl)
    far(0, zl)
    ssq = quarter(0, jnp.zeros((128, 128), F32))
    across()
    near(0, 1 - zl)
    ssq = quarter(1, ssq)
    far(0, 1 - zl)
    ssq = quarter(3, ssq)
    ssq = quarter(2, ssq)
    xp[...] = xacc[:, :D].astype(BF)

    scale = lax.rsqrt(jnp.sum(ssq, axis=-1, keepdims=True) * (1.0 / D) + 1e-06)
    sig = jax.nn.sigmoid(xacc[:, D + 2 * F : D + 2 * F + NE] * scale) * chosen
    total = jnp.sum(sig, axis=-1, keepdims=True)
    this = jnp.sum(jnp.where(iota((128, NE), 1) == e0, sig, 0.0), axis=-1, keepdims=True)
    used = jnp.sum(chosen, axis=-1, keepdims=True) > 0.5
    share = jnp.where(used, this / jnp.where(used, total, 1.0), 0.0)

    def halfmm(cc):
        at = pl.ds(pl.multiple_of(cc * (D // 2), D // 2), D // 2)
        return mm(xp[:, at], gu[pl.ds(8 * cc, 8)].reshape(D // 2, 2 * F))

    both = xacc[:, D : D + 2 * F] + halfmm(c)
    other(0)
    both = (both + halfmm(1 - c)) * scale
    hidden = (jax.nn.silu(both[:, :F]) * both[:, F:] * share).astype(BF)
    hy[:, :F] = hidden
    other(1)
    hy[:, F:] = mm(hidden, dn[...]).astype(BF)

    near_y, far_y = 4 * (y // 4), 4 * (1 - y // 4)
    dests = (
        [far_y + (y + k) % 4 for k in (0, 1, 3, 2)],
        [near_y + (y + k) % 4 for k in (2, 1, 3)],
    )
    for r in (1, 2, 3, 0):
        zz = (zh + r) % NZ
        for i, hb in enumerate((1 - y // 4, y // 4)):
            part = mm(hy[...], ptw[:, pl.ds(pl.multiple_of(zz * ZB + hb * 256, 256), 256)])
            for u in range(2):
                even, odd = part[:64, 128 * u : 128 * u + 128], part[64:, 128 * u : 128 * u + 128]
                outm[zz, 4 * hb + 2 * u] = jnp.where(low, even, pltpu.roll(odd, 64, 1)).astype(BF).reshape(2, CAP, 128)
                outm[zz, 4 * hb + 2 * u + 1] = jnp.where(low, pltpu.roll(even, 64, 1), odd).astype(BF).reshape(2, CAP, 128)
            for to in dests[i]:
                remote(
                    outm.at[zz, to], outr.at[zz, y], osend.at[r], orecv.at[zz], {"tp": zh * NY + to}
                ).start()
        pltpu.make_async_copy(outm.at[zz, y], outr.at[zz, y], orecv.at[zz]).start()

    def sums(r):
        zz = (zh + r) % NZ
        remote(outr.at[zz], outr.at[zz], osend.at[r], orecv.at[zz], ydev(1)).wait_recv()
        got = outr[zz].astype(F32)
        return jnp.stack([jnp.sum(got[:4], axis=0), jnp.sum(got[4:], axis=0)]).astype(BF)

    def pcopy(r, src):
        return remote(zs.at[r], zr.at[src], psend.at[r], precv.at[src], zdev(r))

    for r in (1, 2, 3):
        zs[r] = sums(r)
        pcopy(r, zh).start()
    zr[zh] = sums(0)
    for r in (1, 2, 3):
        pcopy(r, (zh + r) % NZ).wait_recv()

    for j in range(2):
        acc = mm(ctmat[128 * j : 128 * j + 128, :], zr[:, :, j].reshape(256, 128))
        for a in range(2):
            s = 2 * j + a
            out_ref[s] = (
                tok_ref[s].astype(F32) + acc[64 * a : 64 * a + 64, 64 * a : 64 * a + 64]
            ).astype(BF)

    for r in (1, 2, 3):
        zcopy(r, zh).wait_send()
        pcopy(r, zh).wait_send()
    for part in range(2):
        ref = gu.at[pl.ds(0, 15)] if part == 0 else dn.at[:, pl.ds(0, 15 * 128)]
        remote(ref, ref, dsend.at[part], dcore.at[part], peer("core")).wait_send()
    for r in range(NZ):
        ref = xr.at[r, pl.ds(0, NY - 1)]
        remote(ref, ref, ysend.at[r], yrecv.at[r], ydev(1)).wait_send()
        remote(ref, ref, osend.at[r], orecv.at[r], ydev(1)).wait_send()


def body(tokens, norm_gain, router, routes, expert_weights, codes, scales, owner_map):
    dma = pltpu.SemaphoreType.DMA
    vm = pltpu.VMEM
    return pl.pallas_call(
        kernel,
        out_shape=jax.ShapeDtypeStruct(tokens.shape, BF),
        in_specs=[pl.BlockSpec(memory_space=pltpu.HBM)] * 8,
        out_specs=pl.BlockSpec(memory_space=pltpu.VMEM),
        scratch_shapes=[
            vm((4, 64, 64), BF),
            vm((16, 128), BF),
            vm((NE, D), BF),
            vm((4, 2, 64), jnp.int32),
            vm((128, 3 * F), BF),
            vm((48, 128), BF),
            vm((1, D), jnp.int32),
            vm((1, D), F32),
            vm((1, D), jnp.int32),
            vm((D, F), BF),
            vm((16, 128, 2 * F), BF),
            vm((F, D), BF),
            vm((D, D + 2 * F + 128), BF),
            vm((F + D, D), BF),
            vm((128, F + D), BF),
            vm((256, 256), BF),
            vm((256, 256), BF),
            vm((NE, 2, CAP, 128), BF),
            vm((NZ, 2, 2, CAP, 128), BF),
            vm((NZ, NY, 2, CAP, 128), BF),
            vm((128, ZB), BF),
            vm((128, D + 2 * F + 128), F32),
            vm((128, D), BF),
            vm((NZ, NY, 2, CAP, 128), BF),
            vm((NZ, NY, 2, CAP, 128), BF),
            vm((NZ, 2, 2, CAP, 128), BF),
            vm((NZ, 2, 2, CAP, 128), BF),
            dma((9,)), dma((2,)), dma((2, 16, 2)), dma((2,)),
            dma((NZ,)), dma((NZ,)), dma((NZ,)), dma((NZ,)),
            dma((NZ,)), dma((NZ,)), dma((NZ,)), dma((NZ,)),
        ],
        compiler_params=pltpu.CompilerParams(
            collective_id=0, has_side_effects=True, vmem_limit_bytes=60 << 20
        ),
        cost_estimate=pl.CostEstimate(flops=4 * 10**9, bytes_accessed=8 << 20, transcendentals=0),
    )(
        tokens, norm_gain.reshape(16, 128), router.T, routes.transpose(0, 2, 1), expert_weights,
        codes, scales.transpose(0, 2, 1), owner_map.reshape(1, D),
    )


def solution(mesh):
    placed = (
        P(None, ("rep", "fsdp"), "tp"),
        P(),
        P(),
        P(None, ("rep", "fsdp"), None),
        P("tp", None, None),
        P("tp", ("rep", "fsdp"), None),
        P("tp", ("rep", "fsdp"), None),
        P(),
    )
    return jax.shard_map(
        body, mesh=mesh, in_specs=placed, out_specs=P(None, ("rep", "fsdp"), "tp"), check_vma=False
    )
```

```python
import jax
import jax.numpy as jnp
from jax import lax
from jax.experimental import pallas as pl
from jax.experimental.pallas import tpu as pltpu
from jax.sharding import PartitionSpec as P

MESH = pl.DeviceIdType.MESH
BF = jnp.bfloat16
F32 = jnp.float32
NX, NZ, NY, NE, CAP = 4, 4, 8, 8, 32
D, F = 2048, 256
ZB = D // NZ
FAR = (4, 3, 5, 2, 6, 1, 7)


def mm(a, b, ca=1, cb=0):
    return lax.dot_general(a, b, (((ca,), (cb,)), ((), ())), preferred_element_type=F32)


def iota(shape, dim):
    return lax.broadcasted_iota(jnp.int32, shape, dim)


def kernel(
    tok_hbm, gain_hbm, router_hbm, routes_hbm, w_hbm, codes_hbm, scales_hbm, om_hbm, out_ref,
    tok_ref, gain_ref, router_ref, routes_ref, codes_ref, scales_ref, om_ref, grow, omrow,
    wd, gu, dn, wide, ptw, hy, cmat, ctmat, msg, zm, xr, xg, xacc, xp, outm, outr, zs, zr,
    wsem, dsend, drecv, dcore, zsend, zrecv, ysend, yrecv, osend, orecv, psend, precv,
):
    rep, tp, zl = lax.axis_index("rep"), lax.axis_index("tp"), lax.axis_index("fsdp")
    x, c = rep // 2, rep % 2
    zh, y = tp // NY, tp % NY
    e0 = tp // 4
    x1, x2, x3 = (x + 1) % NX, (x + 2) % NX, (x + 3) % NX

    def peer(kind):
        if kind == "core":
            return {"rep": x * 2 + (1 - c)}
        if kind == "z":
            return {"fsdp": 1 - zl}
        return {"rep": (x1 if kind == "up" else x3) * 2 + c}

    def ydev(r):
        return {"tp": zh * NY + (y + r) % NY}

    def zdev(r):
        return {"tp": ((zh + r) % NZ) * NY + y}

    def remote(src, dst, ssem, rsem, dev):
        return pltpu.make_async_remote_copy(
            src_ref=src, dst_ref=dst, send_sem=ssem, recv_sem=rsem, device_id=dev,
            device_id_type=MESH,
        )

    pairs = (
        (scales_hbm.at[0], scales_ref), (codes_hbm.at[0], codes_ref), (routes_hbm, routes_ref),
        (tok_hbm, tok_ref), (om_hbm, om_ref), (router_hbm, router_ref), (gain_hbm, gain_ref),
        (w_hbm.at[0, :, pl.ds(0, 2 * F)], wide.at[:, pl.ds(D, 2 * F)]),
        (w_hbm.at[0, :, pl.ds(2 * F, F)], wd),
    )
    loads = [pltpu.make_async_copy(a, b, wsem.at[i]) for i, (a, b) in enumerate(pairs)]
    loads[0].start()
    loads[1].start()

    bar = pltpu.get_barrier_semaphore()
    partners = [ydev(4), zdev(2), ydev(3), ydev(5), zdev(1), zdev(3)]
    partners += [peer(k) for k in ("z", "up", "down", "core")] + [ydev(r) for r in (2, 6, 1, 7)]
    for dev in partners:
        pl.semaphore_signal(bar, inc=1, device_id=dev, device_id_type=MESH)
    loads[2].start()
    loads[3].start()

    loads[0].wait()
    loads[1].wait()

    def block(cc, xx, zz):
        return cc * 8 + xx * 2 + zz

    def slots(b, n=1):
        return pl.ds(pl.multiple_of(b * 128, 128), n * 128)

    own = block(c, x, zl)
    spread = (iota((48, 768), 1) // 16 == iota((48, 768), 0)).astype(BF)
    delta = codes_ref[...].astype(F32) * mm(scales_ref[...], spread, 0, 0)
    gu[own] = delta[:, : 2 * F].astype(BF)
    dn[:, slots(own)] = delta[:, 2 * F :].T.astype(BF)

    pl.semaphore_wait(bar, len(partners))

    def shard(part, o, h):
        if part == 0:
            return gu.at[o] if h is None else gu.at[o, pl.ds(64 * h, 64)]
        return dn.at[:, slots(o)] if h is None else dn.at[pl.ds(128 * h, 128), slots(o)]

    def send(part, o, h, kind):
        ref = shard(part, o, h)
        sem = dcore.at[part] if kind == "core" else drecv.at[part, o, h]
        remote(ref, ref, dsend.at[part], sem, peer(kind)).start()

    def recv(part, o, h):
        ref = shard(part, o, h)
        remote(ref, ref, dsend.at[part], drecv.at[part, o, h], peer("core")).wait_recv()

    def core(part, o):
        send(part, o, None, "core")

    def over(o):
        remote(shard(1, o, None), shard(1, o, None), dsend.at[1], drecv.at[1, o, 0], peer("z")).start()

    def both_ways(part):
        send(part, own, 0, "up")
        send(part, own, 1, "down")
        send(part, own, 1, "up")
        send(part, own, 0, "down")

    def first():
        send(0, own, 0, "z")
        send(0, own, 1, "z")
        both_ways(1)
        both_ways(0)
        over(own)
        core(1, own)
        core(0, own)

    def pair(part):
        o = block(c, x, 1 - zl)
        recv(part, o, 0)
        send(part, o, 0, "up")
        send(part, o, 0, "down")
        recv(part, o, 1)
        send(part, o, 1, "down")
        send(part, o, 1, "up")

    def onward(part, zz):
        lo, hi = block(c, x3, zz), block(c, x1, zz)
        recv(part, lo, 0)
        send(part, lo, 0, "up")
        recv(part, hi, 1)
        send(part, hi, 1, "down")

    def near(part, zz):
        lo, hi = block(c, x3, zz), block(c, x1, zz)
        recv(part, lo, 1)
        if part == 1:
            over(lo)
        else:
            core(part, lo)
        recv(part, hi, 0)
        if part == 1:
            over(hi)
        else:
            core(part, hi)

    def far(part, zz):
        o = block(c, x2, zz)
        recv(part, o, 0)
        recv(part, o, 1)
        if part == 1:
            over(o)
        core(part, o)

    def across():
        for xx in (x, x3, x1, x2):
            o = block(c, xx, 1 - zl)
            ref = shard(1, o, None)
            remote(ref, ref, dsend.at[1], drecv.at[1, o, 0], peer("core")).wait_recv()
            core(1, o)

    def other(part):
        ref = gu.at[pl.ds(8 * (1 - c), 8)] if part == 0 else dn.at[:, slots(8 * (1 - c), 8)]
        remote(ref, ref, dsend.at[part], dcore.at[part], peer("core")).wait_recv()

    first()
    for cp in loads[4:]:
        cp.start()

    loads[2].wait()
    loads[3].wait()
    lane = iota((256, 128), 1)
    name = iota((128, 64), 0)
    hit = jnp.concatenate(
        [
            ((routes_ref[s, 0:1, :] == name) | (routes_ref[s, 1:2, :] == name)).astype(F32).T
            for s in range(4)
        ],
        axis=0,
    )
    hitb = hit.astype(BF)
    ra, rb = iota((256, 256), 0), iota((256, 256), 1)
    before = ((rb < ra) & (ra // 64 == rb // 64)).astype(BF)
    pos = mm(before, hitb)
    expand = (iota((128, 256), 0) == iota((128, 256), 1) // CAP).astype(BF)
    hitx = mm(hitb, expand)
    posx = mm(pos.astype(BF), expand)
    ct = jnp.where(posx == (rb % CAP).astype(F32), hitx, 0.0)
    ctmat[...] = ct.astype(BF)
    cm = ct.T.astype(BF)
    cmat[...] = cm
    tok = tok_ref[...].reshape(256, 64)
    tok2 = jnp.concatenate([tok, tok], axis=1)
    want = iota((256, 128), 0) // 64
    half = lane // 64
    for j in range(2):
        placed = jnp.where(want == 2 * j + half, tok2.astype(F32), 0.0).astype(BF)
        msg[:, j] = mm(cm, placed).astype(BF).reshape(NE, CAP, 128)

    def zcopy(r, src):
        return remote(msg.at[pl.ds(2 * ((zh + r) % NZ), 2)], zm.at[src], zsend.at[r], zrecv.at[src], zdev(r))

    def zget(r):
        src = (zh + r) % NZ
        zcopy(r, src).wait_recv()
        yput(src)

    def yput(src):
        for r in FAR:
            to = (y + r) % NY
            remote(zm.at[src, to // 4], xr.at[src, y], ysend.at[src], yrecv.at[src], ydev(r)).start()
        pltpu.make_async_copy(zm.at[src, y // 4], xr.at[src, y], yrecv.at[src]).start()

    for r in (1, 3, 2):
        zcopy(r, zh).start()
    zm[zh] = msg[pl.ds(2 * zh, 2)]
    yput(zh)

    for cp in loads[4:7]:
        cp.wait()
    for cc in range(2):
        for xx in range(NX):
            for zz in range(2):
                s = (xx * 2 + cc) * 2 + zz
                b = block(cc, xx, zz)
                omrow[:, 128 * b : 128 * b + 128] = om_ref[:, 128 * s : 128 * s + 128]
    for u in range(16):
        grow[:, 128 * u : 128 * u + 128] = gain_ref[u : u + 1, :].astype(F32)

    def build(lo, hi):
        @pl.loop(lo, hi)
        def _(i):
            base = pl.multiple_of(i * 128, 128)
            wide[pl.ds(base, 128), :D] = jnp.where(
                iota((128, D), 0) + base == omrow[...], 1.0, 0.0
            ).astype(BF)

    def build_back(lo, hi):
        @pl.loop(lo, hi)
        def _(i):
            here = jnp.broadcast_to(omrow[:, slots(i)].astype(F32), (128, 128)).T.astype(jnp.int32)
            rows = pl.ds(pl.multiple_of(F + i * 128, 128), 128)
            for u in range(16):
                ptw[rows, 128 * u : 128 * u + 128] = jnp.where(
                    iota((128, 128), 1) + 128 * u == here, 1.0, 0.0
                ).astype(BF)

    def turn():
        @pl.loop(0, 8)
        def _(i):
            at = pl.ds(pl.multiple_of(i * 256, 256), 256)
            ptw[:F, at] = wd[at, :].astype(F32).T.astype(BF)

    low = iota((64, 128), 1) < 64

    def quarter(r, ssq):
        zz = (zh + r) % NZ
        remote(xr.at[zz], xr.at[zz], ysend.at[zz], yrecv.at[zz], ydev(1)).wait_recv()
        for u in range(NY // 2):
            a = xr[zz, 2 * u].reshape(64, 128).astype(F32)
            b = xr[zz, 2 * u + 1].reshape(64, 128).astype(F32)
            g = grow[:, pl.ds(pl.multiple_of(zz * ZB + 128 * u, 128), 128)]
            even = jnp.where(low, a, pltpu.roll(b, 64, 1))
            odd = jnp.where(low, pltpu.roll(a, 64, 1), b)
            ssq = ssq + jnp.concatenate([even * even, odd * odd], axis=0)
            xg[:64, 128 * u : 128 * u + 128] = (even * g).astype(BF)
            xg[64:, 128 * u : 128 * u + 128] = (odd * g).astype(BF)
        at = pl.ds(pl.multiple_of(zz * ZB, ZB), ZB)
        got = mm(xg[...], wide[at, :])
        if r == 0:
            xacc[...] = got
        else:
            xacc[...] += got
        return ssq

    build(0, 16)
    loads[7].wait()
    loads[8].wait()
    turn()
    for u in range(16):
        names = router_ref[:, 128 * u : 128 * u + 128].astype(F32)
        tall = jnp.concatenate([names, jnp.zeros((128 - NE, 128), F32)], axis=0)
        wide[128 * u : 128 * u + 128, D + 2 * F :] = tall.T.astype(BF)
    mine = cmat[pl.ds(pl.multiple_of(e0 * CAP, CAP), CAP), :].astype(F32)
    four = jnp.concatenate([mine, mine, mine, mine], axis=0)
    rowid = iota((128, 256), 0)
    step = (rowid // 32 % 2) * 2 + rowid // 64
    chosen = mm(jnp.where(iota((128, 256), 1) // 64 == step, four, 0.0).astype(BF), hitb)[:, :NE]
    build_back(0, 8)

    onward(1, zl)
    pair(0)
    near(1, zl)
    onward(0, zl)
    build_back(8, 16)
    core(1, block(c, x3, zl))
    core(1, block(c, x1, zl))
    core(0, block(c, x, 1 - zl))
    zget(1)
    zget(3)
    far(1, zl)
    near(0, zl)
    zget(2)
    onward(0, 1 - zl)
    far(0, zl)
    ssq = quarter(0, jnp.zeros((128, 128), F32))
    across()
    near(0, 1 - zl)
    ssq = quarter(1, ssq)
    far(0, 1 - zl)
    ssq = quarter(3, ssq)
    ssq = quarter(2, ssq)
    xp[...] = xacc[:, :D].astype(BF)

    scale = lax.rsqrt(jnp.sum(ssq, axis=-1, keepdims=True) * (1.0 / D) + 1e-06)
    sig = jax.nn.sigmoid(xacc[:, D + 2 * F : D + 2 * F + NE] * scale) * chosen
    total = jnp.sum(sig, axis=-1, keepdims=True)
    this = jnp.sum(jnp.where(iota((128, NE), 1) == e0, sig, 0.0), axis=-1, keepdims=True)
    used = jnp.sum(chosen, axis=-1, keepdims=True) > 0.5
    share = jnp.where(used, this / jnp.where(used, total, 1.0), 0.0)

    def halfmm(cc):
        at = pl.ds(pl.multiple_of(cc * (D // 2), D // 2), D // 2)
        return mm(xp[:, at], gu[pl.ds(8 * cc, 8)].reshape(D // 2, 2 * F))

    both = xacc[:, D : D + 2 * F] + halfmm(c)
    other(0)
    both = (both + halfmm(1 - c)) * scale
    hidden = (jax.nn.silu(both[:, :F]) * both[:, F:] * share).astype(BF)
    hy[:, :F] = hidden
    other(1)
    hy[:, F:] = mm(hidden, dn[...]).astype(BF)

    near_y, far_y = 4 * (y // 4), 4 * (1 - y // 4)
    dests = (
        [far_y + (y + k) % 4 for k in (0, 1, 3, 2)],
        [near_y + (y + k) % 4 for k in (2, 1, 3)],
    )
    for r in (1, 2, 3, 0):
        zz = (zh + r) % NZ
        for i, hb in enumerate((1 - y // 4, y // 4)):
            part = mm(hy[...], ptw[:, pl.ds(pl.multiple_of(zz * ZB + hb * 256, 256), 256)])
            for u in range(2):
                even, odd = part[:64, 128 * u : 128 * u + 128], part[64:, 128 * u : 128 * u + 128]
                outm[zz, 4 * hb + 2 * u] = jnp.where(low, even, pltpu.roll(odd, 64, 1)).astype(BF).reshape(2, CAP, 128)
                outm[zz, 4 * hb + 2 * u + 1] = jnp.where(low, pltpu.roll(even, 64, 1), odd).astype(BF).reshape(2, CAP, 128)
            for to in dests[i]:
                remote(
                    outm.at[zz, to], outr.at[zz, y], osend.at[r], orecv.at[zz], {"tp": zh * NY + to}
                ).start()
        pltpu.make_async_copy(outm.at[zz, y], outr.at[zz, y], orecv.at[zz]).start()

    def sums(r):
        zz = (zh + r) % NZ
        remote(outr.at[zz], outr.at[zz], osend.at[r], orecv.at[zz], ydev(1)).wait_recv()
        got = outr[zz].astype(F32)
        return jnp.stack([jnp.sum(got[:4], axis=0), jnp.sum(got[4:], axis=0)]).astype(BF)

    def pcopy(r, src):
        return remote(zs.at[r], zr.at[src], psend.at[r], precv.at[src], zdev(r))

    for r in (1, 2, 3):
        zs[r] = sums(r)
        pcopy(r, zh).start()
    zr[zh] = sums(0)
    for r in (1, 2, 3):
        pcopy(r, (zh + r) % NZ).wait_recv()

    for j in range(2):
        acc = mm(ctmat[128 * j : 128 * j + 128, :], zr[:, :, j].reshape(256, 128))
        for a in range(2):
            s = 2 * j + a
            out_ref[s] = (
                tok_ref[s].astype(F32) + acc[64 * a : 64 * a + 64, 64 * a : 64 * a + 64]
            ).astype(BF)

    for r in (1, 2, 3):
        zcopy(r, zh).wait_send()
        pcopy(r, zh).wait_send()
    for part in range(2):
        ref = gu.at[pl.ds(0, 15)] if part == 0 else dn.at[:, pl.ds(0, 15 * 128)]
        remote(ref, ref, dsend.at[part], dcore.at[part], peer("core")).wait_send()
    for r in range(NZ):
        ref = xr.at[r, pl.ds(0, NY - 1)]
        remote(ref, ref, ysend.at[r], yrecv.at[r], ydev(1)).wait_send()
        remote(ref, ref, osend.at[r], orecv.at[r], ydev(1)).wait_send()


def body(tokens, norm_gain, router, routes, expert_weights, codes, scales, owner_map):
    dma = pltpu.SemaphoreType.DMA
    vm = pltpu.VMEM
    return pl.pallas_call(
        kernel,
        out_shape=jax.ShapeDtypeStruct(tokens.shape, BF),
        in_specs=[pl.BlockSpec(memory_space=pltpu.HBM)] * 8,
        out_specs=pl.BlockSpec(memory_space=pltpu.VMEM),
        scratch_shapes=[
            vm((4, 64, 64), BF),
            vm((16, 128), BF),
            vm((NE, D), BF),
            vm((4, 2, 64), jnp.int32),
            vm((128, 3 * F), BF),
            vm((48, 128), BF),
            vm((1, D), jnp.int32),
            vm((1, D), F32),
            vm((1, D), jnp.int32),
            vm((D, F), BF),
            vm((16, 128, 2 * F), BF),
            vm((F, D), BF),
            vm((D, D + 2 * F + 128), BF),
            vm((F + D, D), BF),
            vm((128, F + D), BF),
            vm((256, 256), BF),
            vm((256, 256), BF),
            vm((NE, 2, CAP, 128), BF),
            vm((NZ, 2, 2, CAP, 128), BF),
            vm((NZ, NY, 2, CAP, 128), BF),
            vm((128, ZB), BF),
            vm((128, D + 2 * F + 128), F32),
            vm((128, D), BF),
            vm((NZ, NY, 2, CAP, 128), BF),
            vm((NZ, NY, 2, CAP, 128), BF),
            vm((NZ, 2, 2, CAP, 128), BF),
            vm((NZ, 2, 2, CAP, 128), BF),
            dma((9,)), dma((2,)), dma((2, 16, 2)), dma((2,)),
            dma((NZ,)), dma((NZ,)), dma((NZ,)), dma((NZ,)),
            dma((NZ,)), dma((NZ,)), dma((NZ,)), dma((NZ,)),
        ],
        compiler_params=pltpu.CompilerParams(
            collective_id=0, has_side_effects=True, vmem_limit_bytes=60 << 20
        ),
        cost_estimate=pl.CostEstimate(flops=4 * 10**9, bytes_accessed=8 << 20, transcendentals=0),
    )(
        tokens, norm_gain.reshape(16, 128), router.T, routes.transpose(0, 2, 1), expert_weights,
        codes, scales.transpose(0, 2, 1), owner_map.reshape(1, D),
    )


def solution(mesh):
    placed = (
        P(None, ("rep", "fsdp"), "tp"),
        P(),
        P(),
        P(None, ("rep", "fsdp"), None),
        P("tp", None, None),
        P("tp", ("rep", "fsdp"), None),
        P("tp", ("rep", "fsdp"), None),
        P(),
    )
    return jax.shard_map(
        body, mesh=mesh, in_specs=placed, out_specs=P(None, ("rep", "fsdp"), "tp"), check_vma=False
    )
```

```python
import jax
import jax.numpy as jnp
from jax import lax
from jax.experimental import pallas as pl
from jax.experimental.pallas import tpu as pltpu
from jax.sharding import PartitionSpec as P

MESH = pl.DeviceIdType.MESH
BF = jnp.bfloat16
F32 = jnp.float32
NX, NZ, NY, NE, CAP = 4, 4, 8, 8, 32
D, F = 2048, 256
ZB = D // NZ
FAR = (4, 3, 5, 2, 6, 1, 7)


def mm(a, b, ca=1, cb=0):
    return lax.dot_general(a, b, (((ca,), (cb,)), ((), ())), preferred_element_type=F32)


def iota(shape, dim):
    return lax.broadcasted_iota(jnp.int32, shape, dim)


def kernel(
    tok_hbm, gain_hbm, router_hbm, routes_hbm, w_hbm, codes_hbm, scales_hbm, om_hbm, out_ref,
    tok_ref, gain_ref, router_ref, routes_ref, codes_ref, scales_ref, om_ref, grow, omrow,
    wd, gu, dn, wide, ptw, hy, cmat, ctmat, msg, zm, xr, xg, xacc, xp, outm, outr, zs, zr,
    wsem, dsend, drecv, dcore, zsend, zrecv, ysend, yrecv, osend, orecv, psend, precv,
):
    rep, tp, zl = lax.axis_index("rep"), lax.axis_index("tp"), lax.axis_index("fsdp")
    x, c = rep // 2, rep % 2
    zh, y = tp // NY, tp % NY
    e0 = tp // 4
    x1, x2, x3 = (x + 1) % NX, (x + 2) % NX, (x + 3) % NX

    def peer(kind):
        if kind == "core":
            return {"rep": x * 2 + (1 - c)}
        if kind == "z":
            return {"fsdp": 1 - zl}
        return {"rep": (x1 if kind == "up" else x3) * 2 + c}

    def ydev(r):
        return {"tp": zh * NY + (y + r) % NY}

    def zdev(r):
        return {"tp": ((zh + r) % NZ) * NY + y}

    def remote(src, dst, ssem, rsem, dev):
        return pltpu.make_async_remote_copy(
            src_ref=src, dst_ref=dst, send_sem=ssem, recv_sem=rsem, device_id=dev,
            device_id_type=MESH,
        )

    pairs = (
        (scales_hbm.at[0], scales_ref), (codes_hbm.at[0], codes_ref), (routes_hbm, routes_ref),
        (tok_hbm, tok_ref), (om_hbm, om_ref), (router_hbm, router_ref), (gain_hbm, gain_ref),
        (w_hbm.at[0, :, pl.ds(0, 2 * F)], wide.at[:, pl.ds(D, 2 * F)]),
        (w_hbm.at[0, :, pl.ds(2 * F, F)], wd),
    )
    loads = [pltpu.make_async_copy(a, b, wsem.at[i]) for i, (a, b) in enumerate(pairs)]
    loads[0].start()
    loads[1].start()

    bar = pltpu.get_barrier_semaphore()
    partners = [peer(k) for k in ("z", "up", "down", "core")]
    partners += [ydev(4), zdev(2), ydev(3), ydev(5), zdev(1), zdev(3)]
    partners += [ydev(r) for r in (2, 6, 1, 7)]
    for dev in partners:
        pl.semaphore_signal(bar, inc=1, device_id=dev, device_id_type=MESH)
    loads[2].start()
    loads[3].start()

    loads[0].wait()
    loads[1].wait()

    def block(cc, xx, zz):
        return cc * 8 + xx * 2 + zz

    def slots(b, n=1):
        return pl.ds(pl.multiple_of(b * 128, 128), n * 128)

    own = block(c, x, zl)
    spread = (iota((48, 768), 1) // 16 == iota((48, 768), 0)).astype(BF)
    delta = codes_ref[...].astype(F32) * mm(scales_ref[...], spread, 0, 0)
    gu[own] = delta[:, : 2 * F].astype(BF)
    dn[:, slots(own)] = delta[:, 2 * F :].T.astype(BF)

    pl.semaphore_wait(bar, len(partners))

    def shard(part, o, h):
        if part == 0:
            return gu.at[o] if h is None else gu.at[o, pl.ds(64 * h, 64)]
        return dn.at[:, slots(o)] if h is None else dn.at[pl.ds(128 * h, 128), slots(o)]

    def send(part, o, h, kind):
        ref = shard(part, o, h)
        sem = dcore.at[part] if kind == "core" else drecv.at[part, o, h]
        remote(ref, ref, dsend.at[part], sem, peer(kind)).start()

    def recv(part, o, h):
        ref = shard(part, o, h)
        remote(ref, ref, dsend.at[part], drecv.at[part, o, h], peer("core")).wait_recv()

    def core(part, o):
        send(part, o, None, "core")

    def over(o):
        remote(shard(1, o, None), shard(1, o, None), dsend.at[1], drecv.at[1, o, 0], peer("z")).start()

    def both_ways(part):
        send(part, own, 0, "up")
        send(part, own, 1, "down")
        send(part, own, 1, "up")
        send(part, own, 0, "down")

    def first():
        send(0, own, 0, "z")
        send(0, own, 1, "z")
        both_ways(1)
        both_ways(0)
        over(own)
        core(1, own)
        core(0, own)

    def pair(part):
        o = block(c, x, 1 - zl)
        recv(part, o, 0)
        send(part, o, 0, "up")
        send(part, o, 0, "down")
        recv(part, o, 1)
        send(part, o, 1, "down")
        send(part, o, 1, "up")

    def onward(part, zz):
        lo, hi = block(c, x3, zz), block(c, x1, zz)
        recv(part, lo, 0)
        send(part, lo, 0, "up")
        recv(part, hi, 1)
        send(part, hi, 1, "down")

    def near(part, zz):
        lo, hi = block(c, x3, zz), block(c, x1, zz)
        recv(part, lo, 1)
        if part == 1:
            over(lo)
        else:
            core(part, lo)
        recv(part, hi, 0)
        if part == 1:
            over(hi)
        else:
            core(part, hi)

    def far(part, zz):
        o = block(c, x2, zz)
        recv(part, o, 0)
        recv(part, o, 1)
        if part == 1:
            over(o)
        core(part, o)

    def across():
        for xx in (x, x3, x1, x2):
            o = block(c, xx, 1 - zl)
            ref = shard(1, o, None)
            remote(ref, ref, dsend.at[1], drecv.at[1, o, 0], peer("core")).wait_recv()
            core(1, o)

    def other(part):
        ref = gu.at[pl.ds(8 * (1 - c), 8)] if part == 0 else dn.at[:, slots(8 * (1 - c), 8)]
        remote(ref, ref, dsend.at[part], dcore.at[part], peer("core")).wait_recv()

    first()
    for cp in loads[4:]:
        cp.start()

    loads[2].wait()
    loads[3].wait()
    lane = iota((256, 128), 1)
    name = iota((128, 64), 0)
    hit = jnp.concatenate(
        [
            ((routes_ref[s, 0:1, :] == name) | (routes_ref[s, 1:2, :] == name)).astype(F32).T
            for s in range(4)
        ],
        axis=0,
    )
    hitb = hit.astype(BF)
    ra, rb = iota((256, 256), 0), iota((256, 256), 1)
    before = ((rb < ra) & (ra // 64 == rb // 64)).astype(BF)
    pos = mm(before, hitb)
    expand = (iota((128, 256), 0) == iota((128, 256), 1) // CAP).astype(BF)
    hitx = mm(hitb, expand)
    posx = mm(pos.astype(BF), expand)
    ct = jnp.where(posx == (rb % CAP).astype(F32), hitx, 0.0)
    ctmat[...] = ct.astype(BF)
    cm = ct.T.astype(BF)
    cmat[...] = cm
    tok = tok_ref[...].reshape(256, 64)
    tok2 = jnp.concatenate([tok, tok], axis=1)
    want = iota((256, 128), 0) // 64
    half = lane // 64
    for j in range(2):
        placed = jnp.where(want == 2 * j + half, tok2.astype(F32), 0.0).astype(BF)
        msg[:, j] = mm(cm, placed).astype(BF).reshape(NE, CAP, 128)

    def zcopy(r, src):
        return remote(msg.at[pl.ds(2 * ((zh + r) % NZ), 2)], zm.at[src], zsend.at[r], zrecv.at[src], zdev(r))

    def zget(r):
        src = (zh + r) % NZ
        zcopy(r, src).wait_recv()
        yput(src)

    def yput(src):
        for r in FAR:
            to = (y + r) % NY
            remote(zm.at[src, to // 4], xr.at[src, y], ysend.at[src], yrecv.at[src], ydev(r)).start()
        pltpu.make_async_copy(zm.at[src, y // 4], xr.at[src, y], yrecv.at[src]).start()

    for r in (1, 3, 2):
        zcopy(r, zh).start()
    zm[zh] = msg[pl.ds(2 * zh, 2)]
    yput(zh)

    for cp in loads[4:7]:
        cp.wait()
    for cc in range(2):
        for xx in range(NX):
            for zz in range(2):
                s = (xx * 2 + cc) * 2 + zz
                b = block(cc, xx, zz)
                omrow[:, 128 * b : 128 * b + 128] = om_ref[:, 128 * s : 128 * s + 128]
    for u in range(16):
        grow[:, 128 * u : 128 * u + 128] = gain_ref[u : u + 1, :].astype(F32)

    def build(lo, hi):
        @pl.loop(lo, hi)
        def _(i):
            base = pl.multiple_of(i * 128, 128)
            wide[pl.ds(base, 128), :D] = jnp.where(
                iota((128, D), 0) + base == omrow[...], 1.0, 0.0
            ).astype(BF)

    def build_back(lo, hi):
        @pl.loop(lo, hi)
        def _(i):
            here = jnp.broadcast_to(omrow[:, slots(i)].astype(F32), (128, 128)).T.astype(jnp.int32)
            rows = pl.ds(pl.multiple_of(F + i * 128, 128), 128)
            for u in range(16):
                ptw[rows, 128 * u : 128 * u + 128] = jnp.where(
                    iota((128, 128), 1) + 128 * u == here, 1.0, 0.0
                ).astype(BF)

    def turn():
        @pl.loop(0, 8)
        def _(i):
            at = pl.ds(pl.multiple_of(i * 256, 256), 256)
            ptw[:F, at] = wd[at, :].astype(F32).T.astype(BF)

    low = iota((64, 128), 1) < 64

    def quarter(r, ssq):
        zz = (zh + r) % NZ
        remote(xr.at[zz], xr.at[zz], ysend.at[zz], yrecv.at[zz], ydev(1)).wait_recv()
        for u in range(NY // 2):
            a = xr[zz, 2 * u].reshape(64, 128).astype(F32)
            b = xr[zz, 2 * u + 1].reshape(64, 128).astype(F32)
            g = grow[:, pl.ds(pl.multiple_of(zz * ZB + 128 * u, 128), 128)]
            even = jnp.where(low, a, pltpu.roll(b, 64, 1))
            odd = jnp.where(low, pltpu.roll(a, 64, 1), b)
            ssq = ssq + jnp.concatenate([even * even, odd * odd], axis=0)
            xg[:64, 128 * u : 128 * u + 128] = (even * g).astype(BF)
            xg[64:, 128 * u : 128 * u + 128] = (odd * g).astype(BF)
        at = pl.ds(pl.multiple_of(zz * ZB, ZB), ZB)
        got = mm(xg[...], wide[at, :])
        if r == 0:
            xacc[...] = got
        else:
            xacc[...] += got
        return ssq

    build(0, 16)
    loads[7].wait()
    loads[8].wait()
    turn()
    for u in range(16):
        names = router_ref[:, 128 * u : 128 * u + 128].astype(F32)
        tall = jnp.concatenate([names, jnp.zeros((128 - NE, 128), F32)], axis=0)
        wide[128 * u : 128 * u + 128, D + 2 * F :] = tall.T.astype(BF)
    mine = cmat[pl.ds(pl.multiple_of(e0 * CAP, CAP), CAP), :].astype(F32)
    four = jnp.concatenate([mine, mine, mine, mine], axis=0)
    rowid = iota((128, 256), 0)
    step = (rowid // 32 % 2) * 2 + rowid // 64
    chosen = mm(jnp.where(iota((128, 256), 1) // 64 == step, four, 0.0).astype(BF), hitb)[:, :NE]
    build_back(0, 8)

    onward(1, zl)
    pair(0)
    near(1, zl)
    onward(0, zl)
    build_back(8, 16)
    core(1, block(c, x3, zl))
    core(1, block(c, x1, zl))
    core(0, block(c, x, 1 - zl))
    zget(1)
    zget(3)
    far(1, zl)
    near(0, zl)
    zget(2)
    onward(0, 1 - zl)
    far(0, zl)
    ssq = quarter(0, jnp.zeros((128, 128), F32))
    across()
    near(0, 1 - zl)
    ssq = quarter(1, ssq)
    far(0, 1 - zl)
    ssq = quarter(3, ssq)
    ssq = quarter(2, ssq)
    xp[...] = xacc[:, :D].astype(BF)

    scale = lax.rsqrt(jnp.sum(ssq, axis=-1, keepdims=True) * (1.0 / D) + 1e-06)
    sig = jax.nn.sigmoid(xacc[:, D + 2 * F : D + 2 * F + NE] * scale) * chosen
    total = jnp.sum(sig, axis=-1, keepdims=True)
    this = jnp.sum(jnp.where(iota((128, NE), 1) == e0, sig, 0.0), axis=-1, keepdims=True)
    used = jnp.sum(chosen, axis=-1, keepdims=True) > 0.5
    share = jnp.where(used, this / jnp.where(used, total, 1.0), 0.0)

    def halfmm(cc):
        at = pl.ds(pl.multiple_of(cc * (D // 2), D // 2), D // 2)
        return mm(xp[:, at], gu[pl.ds(8 * cc, 8)].reshape(D // 2, 2 * F))

    both = xacc[:, D : D + 2 * F] + halfmm(c)
    other(0)
    both = (both + halfmm(1 - c)) * scale
    hidden = (jax.nn.silu(both[:, :F]) * both[:, F:] * share).astype(BF)
    hy[:, :F] = hidden
    other(1)
    hy[:, F:] = mm(hidden, dn[...]).astype(BF)

    near_y, far_y = 4 * (y // 4), 4 * (1 - y // 4)
    dests = (
        [far_y + (y + k) % 4 for k in (0, 1, 3, 2)],
        [near_y + (y + k) % 4 for k in (2, 1, 3)],
    )
    for r in (1, 2, 3, 0):
        zz = (zh + r) % NZ
        for i, hb in enumerate((1 - y // 4, y // 4)):
            part = mm(hy[...], ptw[:, pl.ds(pl.multiple_of(zz * ZB + hb * 256, 256), 256)])
            for u in range(2):
                even, odd = part[:64, 128 * u : 128 * u + 128], part[64:, 128 * u : 128 * u + 128]
                outm[zz, 4 * hb + 2 * u] = jnp.where(low, even, pltpu.roll(odd, 64, 1)).astype(BF).reshape(2, CAP, 128)
                outm[zz, 4 * hb + 2 * u + 1] = jnp.where(low, pltpu.roll(even, 64, 1), odd).astype(BF).reshape(2, CAP, 128)
            for to in dests[i]:
                remote(
                    outm.at[zz, to], outr.at[zz, y], osend.at[r], orecv.at[zz], {"tp": zh * NY + to}
                ).start()
        pltpu.make_async_copy(outm.at[zz, y], outr.at[zz, y], orecv.at[zz]).start()

    def sums(r):
        zz = (zh + r) % NZ
        remote(outr.at[zz], outr.at[zz], osend.at[r], orecv.at[zz], ydev(1)).wait_recv()
        got = outr[zz].astype(F32)
        return jnp.stack([jnp.sum(got[:4], axis=0), jnp.sum(got[4:], axis=0)]).astype(BF)

    def pcopy(r, src):
        return remote(zs.at[r], zr.at[src], psend.at[r], precv.at[src], zdev(r))

    for r in (1, 2, 3):
        zs[r] = sums(r)
        pcopy(r, zh).start()
    zr[zh] = sums(0)
    for r in (1, 2, 3):
        pcopy(r, (zh + r) % NZ).wait_recv()

    for j in range(2):
        acc = mm(ctmat[128 * j : 128 * j + 128, :], zr[:, :, j].reshape(256, 128))
        for a in range(2):
            s = 2 * j + a
            out_ref[s] = (
                tok_ref[s].astype(F32) + acc[64 * a : 64 * a + 64, 64 * a : 64 * a + 64]
            ).astype(BF)

    for r in (1, 2, 3):
        zcopy(r, zh).wait_send()
        pcopy(r, zh).wait_send()
    for part in range(2):
        ref = gu.at[pl.ds(0, 15)] if part == 0 else dn.at[:, pl.ds(0, 15 * 128)]
        remote(ref, ref, dsend.at[part], dcore.at[part], peer("core")).wait_send()
    for r in range(NZ):
        ref = xr.at[r, pl.ds(0, NY - 1)]
        remote(ref, ref, ysend.at[r], yrecv.at[r], ydev(1)).wait_send()
        remote(ref, ref, osend.at[r], orecv.at[r], ydev(1)).wait_send()


def body(tokens, norm_gain, router, routes, expert_weights, codes, scales, owner_map):
    dma = pltpu.SemaphoreType.DMA
    vm = pltpu.VMEM
    return pl.pallas_call(
        kernel,
        out_shape=jax.ShapeDtypeStruct(tokens.shape, BF),
        in_specs=[pl.BlockSpec(memory_space=pltpu.HBM)] * 8,
        out_specs=pl.BlockSpec(memory_space=pltpu.VMEM),
        scratch_shapes=[
            vm((4, 64, 64), BF),
            vm((16, 128), BF),
            vm((NE, D), BF),
            vm((4, 2, 64), jnp.int32),
            vm((128, 3 * F), BF),
            vm((48, 128), BF),
            vm((1, D), jnp.int32),
            vm((1, D), F32),
            vm((1, D), jnp.int32),
            vm((D, F), BF),
            vm((16, 128, 2 * F), BF),
            vm((F, D), BF),
            vm((D, D + 2 * F + 128), BF),
            vm((F + D, D), BF),
            vm((128, F + D), BF),
            vm((256, 256), BF),
            vm((256, 256), BF),
            vm((NE, 2, CAP, 128), BF),
            vm((NZ, 2, 2, CAP, 128), BF),
            vm((NZ, NY, 2, CAP, 128), BF),
            vm((128, ZB), BF),
            vm((128, D + 2 * F + 128), F32),
            vm((128, D), BF),
            vm((NZ, NY, 2, CAP, 128), BF),
            vm((NZ, NY, 2, CAP, 128), BF),
            vm((NZ, 2, 2, CAP, 128), BF),
            vm((NZ, 2, 2, CAP, 128), BF),
            dma((9,)), dma((2,)), dma((2, 16, 2)), dma((2,)),
            dma((NZ,)), dma((NZ,)), dma((NZ,)), dma((NZ,)),
            dma((NZ,)), dma((NZ,)), dma((NZ,)), dma((NZ,)),
        ],
        compiler_params=pltpu.CompilerParams(
            collective_id=0, has_side_effects=True, vmem_limit_bytes=60 << 20
        ),
        cost_estimate=pl.CostEstimate(flops=4 * 10**9, bytes_accessed=8 << 20, transcendentals=0),
    )(
        tokens, norm_gain.reshape(16, 128), router.T, routes.transpose(0, 2, 1), expert_weights,
        codes, scales.transpose(0, 2, 1), owner_map.reshape(1, D),
    )


def solution(mesh):
    placed = (
        P(None, ("rep", "fsdp"), "tp"),
        P(),
        P(),
        P(None, ("rep", "fsdp"), None),
        P("tp", None, None),
        P("tp", ("rep", "fsdp"), None),
        P("tp", ("rep", "fsdp"), None),
        P(),
    )
    return jax.shard_map(
        body, mesh=mesh, in_specs=placed, out_specs=P(None, ("rep", "fsdp"), "tp"), check_vma=False
    )
```
